512 devices in a mesh: img: 8 (over x, core), cls: 8 (over z_lo), tpl: 8 (over z_hi, y).
Axes of the slice: x: 4, y: 4, z: 16 (z_hi: 2, z_lo: 8; z = z_hi * 8 + z_lo), core: 2. Of those that a mesh axis runs over, the one named last changes fastest.
Arguments:
- images: bfloat16 [16384, 1280], P(('img', 'tpl')), may hold values from -5 to 5
- labels: int32 [16384], P(('img', 'tpl')), may hold values from 0 to 4095
- templates: bfloat16 [32, 4096, 1280], P('tpl', ('cls', 'img')), may hold values from -0.125 to 0.125
- projection: bfloat16 [1280, 1280], P('img', 'cls'), may hold values from -0.08441157 to 0.08441157
Outputs:
- grad_templates: bfloat16 [32, 4096, 1280], P('tpl', ('cls', 'img'))
- grad_projection: float32 [1280, 1280], P('img', 'cls')
The draws below stay inside these ranges and needn't reach their ends.
All inputs are finite; a program needn't handle non-finite values.
Results may differ from the reference program's by a relative error of at most 0.011.
Values may be sent and summed in bfloat16 or wider, within the bound.
A program may use at most 64 MiB of HBM per device.

```python
import math
import jax
import jax.numpy as jnp
from jax import lax

D = 1280
C = 4096
TEMPLATES = 32
IMAGES = 16384


def noise_field(seed_key, shape):
    return jax.random.normal(seed_key, shape, jnp.float32)


def label_draw(key):
    drawn = jax.random.randint(jax.random.fold_in(key, 11), (IMAGES,), 0, C, dtype=jnp.int32)
    first_slot = jax.random.randint(jax.random.fold_in(key, 12), (), 0, IMAGES, dtype=jnp.int32)
    offset_slot = jax.random.randint(jax.random.fold_in(key, 13), (), 1, IMAGES, dtype=jnp.int32)
    second_slot = (first_slot + offset_slot) % IMAGES
    drawn = drawn.at[first_slot].set(C - 1)
    drawn = drawn.at[second_slot].set(0)
    return drawn.astype(jnp.int32)


def domain_basis(key):
    return jax.random.normal(jax.random.fold_in(key, 24), (8, D), jnp.float32)


def class_latent(key):
    group_count = C // 8
    single_part = noise_field(jax.random.fold_in(key, 21), (C, D))
    group_rows = noise_field(jax.random.fold_in(key, 22), (group_count, D))
    sibling_part = jnp.tile(group_rows, (8, 1))
    loading = jax.random.normal(jax.random.fold_in(key, 23), (C, 8), jnp.float32)
    basis_rows = domain_basis(key)
    domain_part = jnp.dot(loading, basis_rows, precision=lax.Precision.HIGHEST) / math.sqrt(8.0)
    return 0.632 * single_part + 0.548 * sibling_part + 0.548 * domain_part


def projection_matrix(key):
    raw_values = jax.random.normal(jax.random.fold_in(key, 31), (D, D), jnp.float32)
    return jnp.clip(raw_values, -3.0, 3.0) / math.sqrt(D)


def draw_labels(key, part):
    return label_draw(key)


def draw_projection(key, part):
    return projection_matrix(key).astype(jnp.bfloat16)


def draw_templates(key, part):
    latent = class_latent(key)
    basis_rows = domain_basis(key)
    style_coef = jax.random.normal(jax.random.fold_in(key, 52), (TEMPLATES, 8), jnp.float32)
    style_rows = jnp.dot(style_coef, basis_rows, precision=lax.Precision.HIGHEST) / math.sqrt(8.0)
    row_scale = jax.random.uniform(jax.random.fold_in(key, 53), (TEMPLATES, C, 1), jnp.float32, 0.4, 1.6)
    spread_noise = noise_field(jax.random.fold_in(key, 51), (TEMPLATES, C, D))
    mixture = 0.45 * latent[None] + 0.6 * spread_noise + 0.6 * style_rows[:, None, :]
    return jnp.clip(0.022 * row_scale * mixture, -0.12, 0.12).astype(jnp.bfloat16)


def draw_images(key, part):
    class_ids = label_draw(key)
    latent = class_latent(key)
    proj_values = projection_matrix(key)
    directions = jnp.dot(latent, proj_values, precision=lax.Precision.HIGHEST)
    directions = directions / jnp.sqrt(jnp.sum(directions * directions, axis=1, keepdims=True) + 1e-06)
    picked = jnp.take(directions, class_ids, axis=0)
    strength = jax.random.uniform(jax.random.fold_in(key, 43), (IMAGES, 1), jnp.float32, 0.15, 0.7)
    image_noise = noise_field(jax.random.fold_in(key, 41), (IMAGES, D))
    values = strength * math.sqrt(D) * picked + image_noise
    return jnp.clip(values, -5.0, 5.0).astype(jnp.bfloat16)


def setup_inputs(seed: int = 0) -> dict:
    keys = jax.random.split(jax.random.key(seed), 5)
    images = draw_images(jax.random.fold_in(keys[4], 71), 0)
    labels = draw_labels(jax.random.fold_in(keys[4], 71), 0)
    templates = draw_templates(jax.random.fold_in(keys[4], 71), 0)
    projection = draw_projection(jax.random.fold_in(keys[4], 71), 0)
    return {"images": images, "labels": labels, "templates": templates, "projection": projection}


logit_scale = 50.0
epsilon = 1e-06

def inverse_norm(values):
    return lax.rsqrt(lax.optimization_barrier(jnp.sum(values * values, axis=-1, keepdims=True)) + epsilon)

def reference(images, labels, templates, projection):
    flat_tpl = templates.reshape(TEMPLATES * C, D)
    text_z = jnp.dot(flat_tpl, projection, preferred_element_type=jnp.float32)
    text_rz = inverse_norm(text_z)
    text_u = text_z * text_rz
    mean_emb = lax.optimization_barrier(jnp.sum(text_u.reshape(TEMPLATES, C, D), axis=0)) / TEMPLATES
    mean_rn = inverse_norm(mean_emb)
    class_w = mean_emb * mean_rn
    class_b = class_w.astype(jnp.bfloat16)
    img_f = images.astype(jnp.float32)
    img_b = (img_f * inverse_norm(img_f)).astype(jnp.bfloat16)
    scores = logit_scale * jnp.dot(img_b, class_b.T, preferred_element_type=jnp.float32)
    exp_scores = jnp.exp(scores)
    totals = lax.optimization_barrier(jnp.sum(exp_scores, axis=1, keepdims=True))
    class_ids = jnp.arange(C, dtype=jnp.int32)
    one_hot = (labels[:, None] == class_ids[None, :]).astype(jnp.float32)
    grad_logit = (exp_scores / totals - one_hot).astype(jnp.bfloat16)
    class_g = logit_scale * jnp.dot(grad_logit.T, img_b, preferred_element_type=jnp.float32)
    dot_wg = lax.optimization_barrier(jnp.sum(class_w * class_g, axis=1, keepdims=True))
    grad_mean = (class_g - class_w * dot_wg) * mean_rn
    per_u = grad_mean / TEMPLATES
    u_three = text_u.reshape(TEMPLATES, C, D)
    inner_prod = lax.optimization_barrier(jnp.sum(u_three * per_u[None], axis=2, keepdims=True))
    grad_z = ((per_u[None] - u_three * inner_prod) * text_rz.reshape(TEMPLATES, C, 1)).astype(jnp.bfloat16)
    grad_flat = grad_z.reshape(TEMPLATES * C, D)
    grad_templates = jnp.dot(grad_flat, projection.T, preferred_element_type=jnp.float32).astype(jnp.bfloat16)
    grad_projection = jnp.dot(flat_tpl.T, grad_flat, preferred_element_type=jnp.float32)
    return (grad_templates.reshape(TEMPLATES, C, D), grad_projection)
```

```python
import jax
import jax.numpy as jnp
from jax import lax
from jax.experimental import pallas as pl
from jax.experimental.pallas import tpu as pltpu
from jax.sharding import PartitionSpec as P

SCALE = 50.0
EPS = 1e-06
TPL = 32
MESH = pl.DeviceIdType.MESH
BF = jnp.bfloat16
F32 = jnp.float32
PLANE = [(a, b) for a in range(4) for b in range(4) if (a, b) != (0, 0)]
RING = (4, -4, 3, -3, 2, -2, 1, -1)


def inv_norm(v):
    return lax.rsqrt(jnp.sum(v * v, axis=-1, keepdims=True) + EPS)


def device(x, k, y, zh, zl):
    return (x * 2 + k, zl, zh * 4 + y)


class Copies:
    def __init__(self, send, recv):
        self.send, self.recv, self.used = send, recv, 0
        self.open = []

    def __call__(self, src, dst, to):
        n = self.used
        self.used += 1
        cp = pltpu.make_async_remote_copy(
            src_ref=src, dst_ref=dst, send_sem=self.send.at[n], recv_sem=self.recv.at[n],
            device_id=to, device_id_type=MESH)
        cp.start()
        self.open.append(cp)
        return cp

    def finish(self):
        for cp in self.open:
            cp.wait_send()


N_COPIES = 120


def kernel(images, labels, tpl, tplt, proj, gt_out, gp_out,
           wf, pk, pf, zbuf, rzbuf, s_send, s_recv, c_send, c_recv, mbuf, cb, img, lab,
           ebuf, e_send, e_one, e_two, e_recv, gbuf, cg_send, cg_recv, f_send, f_recv, gs, gz, tx,
           hs, hr, rs, w_recv, h_send, h_recv, hy, send_sem, recv_sem):
    i = lax.axis_index("img")
    c = lax.axis_index("cls")
    t = lax.axis_index("tpl")
    x, k, y, zh = i // 2, i % 2, t % 4, t // 4
    z = zh * 8 + c
    other = 1 - k

    def at_plane(dx, dy):
        return (x + dx) % 4, (y + dy) % 4

    def to_plane(dx, dy):
        px, py = at_plane(dx, dy)
        return device(px, k, py, zh, c)

    def to_ring(d):
        n = (z + d + 16) % 16
        return device(x, k, y, n // 8, n % 8)

    sibling = device(x, other, y, zh, c)
    across = device(x, k, y, 1 - zh, c)

    barrier = pltpu.get_barrier_semaphore()
    for dx, dy in PLANE:
        pl.semaphore_signal(barrier, inc=1, device_id=to_plane(dx, dy), device_id_type=MESH)
    for d in range(1, 16):
        pl.semaphore_signal(barrier, inc=1, device_id=to_ring(d), device_id_type=MESH)
    pl.semaphore_signal(barrier, inc=1, device_id=sibling, device_id_type=MESH)

    copy = Copies(send_sem, recv_sem)

    wf[...] = jnp.zeros_like(wf)
    wf[:, 0:160] = proj[...].astype(F32)
    pk[c] = pltpu.roll(wf[...], 32 * (c % 4), 1).astype(BF)

    pl.semaphore_wait(barrier, 31)

    cols = []
    for d in RING:
        if d == 4:
            part = pk.at[c, pl.ds(0, 80)]
        elif d == -4:
            part = pk.at[c, pl.ds(80, 80)]
        else:
            part = pk.at[c]
        cols.append(copy(part, part, to_ring(d)))

    img_f = images[...].astype(F32)
    img[k] = (img_f * inv_norm(img_f)).astype(BF)
    lab[k] = labels[...]
    to_img = copy(img.at[k], img.at[k], sibling)
    to_lab = copy(lab.at[k], lab.at[k], sibling)
    to_tx = copy(tplt.at[other], tx, sibling)

    for cp in cols:
        cp.wait_recv()
    for h in range(2):
        b = h * 4
        tiles = [
            pk[b, :, 0:128],
            pk[b, :, 128:256] + pk[b + 1, :, 0:128],
            pk[b + 1, :, 128:256] + pk[b + 2, :, 0:128],
            pk[b + 2, :, 128:256] + pk[b + 3, :, 0:128],
            pk[b + 3, :, 128:256],
        ]
        for j, tile in enumerate(tiles):
            o = (h * 5 + j) * 128
            pf[i, :, o:o + 128] = tile

    rows = [copy(pf.at[i], pf.at[i], device((x + dx) % 4, k, y, zh, c)) for dx in (1, 3, 2)]
    shared = [copy(pf.at[i], pf.at[i], sibling)]
    for dx, cp in zip((1, 3, 2), rows):
        cp.wait_recv()
        src = ((x - dx + 4) % 4) * 2 + k
        shared.append(copy(pf.at[src], pf.at[src], sibling))
    for cp in shared:
        cp.wait_recv()

    def project(n, _):
        o = pl.ds(pl.multiple_of(n * 256, 256), 256)
        zbuf[:, o] = jnp.dot(tpl[...], pf[:, :, o].reshape(1280, 256), preferred_element_type=F32)
        return 0
    lax.fori_loop(0, 5, project, 0)
    rz = inv_norm(zbuf[...])
    rzbuf[...] = rz
    zbuf[...] = zbuf[...] * rz
    total = zbuf[0:64] + zbuf[64:128] + zbuf[128:192] + zbuf[192:256]
    s_send[...] = total.astype(BF).reshape(4, 16, 1280)

    got = [copy(s_send.at[(y + d) % 4], s_recv.at[d - 1], to_plane(0, d)) for d in (2, 1, 3)]
    for cp in got:
        cp.wait_recv()
    own = s_send[y].astype(F32)
    for d in range(3):
        own = own + s_recv[d].astype(F32)
    c_send[...] = own.astype(BF)
    copy(c_send, c_recv, across).wait_recv()
    mbuf[x, y] = ((c_send[...].astype(F32) + c_recv[...].astype(F32)) / TPL).astype(BF)

    got = [copy(mbuf.at[x, y], mbuf.at[x, y], to_plane(dx, dy)) for dx, dy in PLANE]
    to_img.wait_recv()
    to_lab.wait_recv()
    to_tx.wait_recv()
    for cp in got:
        cp.wait_recv()

    mean = mbuf[...].reshape(256, 1280).astype(F32)
    cb[...] = (mean * inv_norm(mean)).astype(BF)
    for s in range(2):
        sc = lax.dot_general(cb[...], img[s], (((1,), (1,)), ((), ())), preferred_element_type=F32)
        ebuf[:, s * 256:(s + 1) * 256] = jnp.exp(SCALE * sc)
    e_send[...] = jnp.sum(ebuf[...].reshape(32, 8, 512), axis=0)
    copy(e_send, e_one, sibling).wait_recv()
    e_two[...] = e_send[...] + e_one[...]
    got = [copy(e_two, e_recv.at[d - 1], device(x, k, y, zh, (c + d) % 8)) for d in range(1, 8)]
    row = lax.broadcasted_iota(jnp.int32, (256, 1), 0)
    ids = (c * 8 + (row // 64) * 2 + k) * 64 + row % 64
    for cp in got:
        cp.wait_recv()
    tot = e_two[...]
    for d in range(7):
        tot = tot + e_recv[d]
    inv = 1.0 / jnp.sum(tot, axis=0, keepdims=True)
    for s in range(2):
        part = slice(s * 256, (s + 1) * 256)
        hot = (lab[s, 0:1, :] == ids).astype(F32)
        gbuf[:, part] = (ebuf[:, part] * inv[:, part] - hot).astype(BF)

    def class_grad(n, _):
        o = pl.ds(pl.multiple_of(n * 256, 256), 256)
        v = jnp.dot(gbuf[...], img[:, :, o].reshape(512, 256), preferred_element_type=F32)
        cg_send[:, :, :, o] = (SCALE * v).astype(BF).reshape(4, 4, 16, 256)
        return 0
    lax.fori_loop(0, 5, class_grad, 0)

    got = []
    for n, (dx, dy) in enumerate(PLANE):
        px, py = at_plane(dx, dy)
        got.append(copy(cg_send.at[px, py], cg_recv.at[n], to_plane(dx, dy)))
    for cp in got:
        cp.wait_recv()
    own = cg_send[x, y].astype(F32)
    for n in range(15):
        own = own + cg_recv[n].astype(F32)
    f_send[...] = own.astype(BF)
    copy(f_send, f_recv, across).wait_recv()
    gs[y] = (f_send[...].astype(F32) + f_recv[...].astype(F32)).astype(BF)
    got = [copy(gs.at[y], gs.at[y], to_plane(0, d)) for d in (2, 1, 3)]
    mean = mbuf[x].reshape(64, 1280).astype(F32)
    rn = inv_norm(mean)
    class_w = mean * rn
    for cp in got:
        cp.wait_recv()

    class_g = gs[...].reshape(64, 1280).astype(F32)
    dot_wg = jnp.sum(class_w * class_g, axis=1, keepdims=True)
    per_u = (class_g - class_w * dot_wg) * rn / TPL
    for n in range(4):
        rows_n = slice(n * 64, (n + 1) * 64)
        u = zbuf[rows_n]
        inner = jnp.sum(u * per_u, axis=1, keepdims=True)
        gz[k, rows_n] = ((per_u - u * inner) * rzbuf[rows_n]).astype(BF)

    copy(gz.at[k], gz.at[k], sibling).wait_recv()

    got = []
    for dx in (2, 1, 3, 0):
        px = (x + dx) % 4

        def product(n, _):
            o = pl.ds(pl.multiple_of(n * 256, 256), 256)
            v = jnp.dot(tplt[k, px], gz[k, :, o], preferred_element_type=F32)
            v = v + jnp.dot(tx[px], gz[other, :, o], preferred_element_type=F32)
            hs[px, :, o] = v.astype(BF)
            return 0
        lax.fori_loop(0, 5, product, 0)
        for dy in (2, 1, 3, 0):
            if (dx, dy) == (0, 0):
                continue
            py = (y + dy) % 4
            start = pl.multiple_of(jnp.minimum(48 * py, 112), 16)
            got.append(copy(hs.at[px, pl.ds(start, 48)], hr.at[PLANE.index((dx, dy))], to_plane(dx, dy)))

    for m in range(4):
        w = pf[2 * m:2 * m + 2].reshape(320, 1280)
        v = lax.dot_general(gz[k], w, (((1,), (1,)), ((), ())), preferred_element_type=F32)
        gt_out[:, m * 320:(m + 1) * 320] = v.astype(BF)

    for cp in got:
        cp.wait_recv()
    own = hs[x, pl.ds(pl.multiple_of(jnp.minimum(48 * y, 112), 16), 48)].astype(F32)
    for n in range(15):
        own = own + hr[n].astype(F32)
    rs[...] = own.astype(BF)

    def window(cc):
        return pl.ds(pl.multiple_of(128 * ((5 * cc) // 4), 128), 256)

    got = []
    for n, d in enumerate((4, 3, -3, 2, -2, 1, -1)):
        got.append(copy(rs.at[:, window((c + d + 8) % 8)], w_recv.at[n], to_ring(d)))
    for cp in got:
        cp.wait_recv()
    own = rs[:, window(c)].astype(F32)
    for n in range(7):
        own = own + w_recv[n].astype(F32)
    h_send[...] = own.astype(BF)
    copy(h_send, h_recv, across).wait_recv()
    hy[y] = (h_send[...].astype(F32) + h_recv[...].astype(F32)).astype(BF)
    got = [copy(hy.at[y], hy.at[y], to_plane(0, d)) for d in (2, 1, 3)]
    for cp in got:
        cp.wait_recv()
    for n in range(4):
        v = pltpu.roll(hy[n].astype(F32), (256 - 32 * (c % 4)) % 256, 1)[:, 0:160]
        if n < 3:
            gp_out[48 * n:48 * n + 48] = v
        else:
            gp_out[144:160] = v[32:48]
    copy.finish()


def body(images, labels, templates, projection):
    flat = templates.reshape(256, 1280)
    tplt = flat.T.reshape(4, 2, 160, 256).transpose(1, 0, 2, 3)
    lab = jnp.broadcast_to(labels.reshape(1, 256), (8, 256))
    vm = pl.BlockSpec(memory_space=pltpu.VMEM)
    scratch = [
        ((160, 256), F32), ((8, 160, 256), BF), ((8, 160, 1280), BF), ((256, 1280), F32), ((256, 1), F32),
        ((4, 16, 1280), BF), ((3, 16, 1280), BF), ((16, 1280), BF), ((16, 1280), BF),
        ((4, 4, 16, 1280), BF), ((256, 1280), BF), ((2, 256, 1280), BF), ((2, 8, 256), jnp.int32),
        ((256, 512), F32), ((8, 512), F32), ((8, 512), F32), ((8, 512), F32), ((7, 8, 512), F32),
        ((256, 512), BF), ((4, 4, 16, 1280), BF), ((15, 16, 1280), BF), ((16, 1280), BF), ((16, 1280), BF),
        ((4, 16, 1280), BF), ((2, 256, 1280), BF), ((4, 160, 256), BF),
        ((4, 160, 1280), BF), ((15, 48, 1280), BF), ((48, 1280), BF), ((7, 48, 256), BF),
        ((48, 256), BF), ((48, 256), BF), ((4, 48, 256), BF),
    ]
    gt, gp = pl.pallas_call(
        kernel,
        out_shape=(jax.ShapeDtypeStruct((256, 1280), BF), jax.ShapeDtypeStruct((160, 160), F32)),
        in_specs=[vm] * 5,
        out_specs=(vm, vm),
        scratch_shapes=[pltpu.VMEM(s, d) for s, d in scratch]
        + [pltpu.SemaphoreType.DMA((N_COPIES,)), pltpu.SemaphoreType.DMA((N_COPIES,))],
        compiler_params=pltpu.CompilerParams(
            collective_id=0, has_side_effects=True, vmem_limit_bytes=50 << 20),
    )(images, lab, flat, tplt, projection)
    return gt.reshape(templates.shape), gp


def solution(mesh):
    in_specs = (
        P(("img", "tpl"), None),
        P(("img", "tpl")),
        P("tpl", ("cls", "img"), None),
        P("img", "cls"),
    )
    out_specs = (P("tpl", ("cls", "img"), None), P("img", "cls"))
    return jax.shard_map(body, mesh=mesh, in_specs=in_specs, out_specs=out_specs, check_vma=False)
```

```python
import jax
import jax.numpy as jnp
from jax import lax
from jax.experimental import pallas as pl
from jax.experimental.pallas import tpu as pltpu
from jax.sharding import PartitionSpec as P

SCALE = 50.0
EPS = 1e-06
TPL = 32
MESH = pl.DeviceIdType.MESH
BF = jnp.bfloat16
F32 = jnp.float32
PLANE = [(a, b) for a in range(4) for b in range(4) if (a, b) != (0, 0)]
RING = (4, -4, 3, -3, 2, -2, 1, -1)


def inv_norm(v):
    return lax.rsqrt(jnp.sum(v * v, axis=-1, keepdims=True) + EPS)


def device(x, k, y, zh, zl):
    return (x * 2 + k, zl, zh * 4 + y)


class Copies:
    def __init__(self, send, recv):
        self.send, self.recv, self.used = send, recv, 0
        self.open = []

    def __call__(self, src, dst, to):
        n = self.used
        self.used += 1
        cp = pltpu.make_async_remote_copy(
            src_ref=src, dst_ref=dst, send_sem=self.send.at[n], recv_sem=self.recv.at[n],
            device_id=to, device_id_type=MESH)
        cp.start()
        self.open.append(cp)
        return cp

    def finish(self):
        for cp in self.open:
            cp.wait_send()


N_COPIES = 130
NEAR = (4, 3, -3, 2, -2, 1, -1)


def kernel(images, labels, tpl, proj, gt_out, gp_out,
           wf, pw, zb, pf, tt, zbuf, rzbuf, s_send, s_recv, c_send, c_recv, mbuf, cb, img, lab,
           ebuf, e_send, e_one, e_two, e_recv, gbuf, cg_send, cg_recv, f_send, f_recv, gs, gz, gx,
           hs, hr, h2, h2r, rs, w_recv, h_send, h_recv, hp, hy,
           send_sem, recv_sem, z_send, z_recv, w_send, w_recv_sem, y_send, y_recv):
    i = lax.axis_index("img")
    c = lax.axis_index("cls")
    t = lax.axis_index("tpl")
    x, k, y, zh = i // 2, i % 2, t % 4, t // 4
    z = zh * 8 + c
    other = 1 - k
    row_core, col_core = y // 2, c // 4

    def at_plane(dx, dy):
        return (x + dx) % 4, (y + dy) % 4

    def to_plane(dx, dy):
        px, py = at_plane(dx, dy)
        return device(px, k, py, zh, c)

    def to_z(n, core):
        n = (n + 16) % 16
        return device(x, core, y, n // 8, n % 8)

    def to_first(d):
        return device((x + d * other) % 4, k, (y + d * k) % 4, zh, c)

    def to_second(d):
        return device((x + d * k) % 4, k, (y + d * other) % 4, zh, c)

    def place(first, second):
        return first * other + second * k, second * other + first * k

    first, second = place(x, y)
    sibling = device(x, other, y, zh, c)
    across = device(x, k, y, 1 - zh, c)

    barrier = pltpu.get_barrier_semaphore()
    peers = [to_plane(dx, dy) for dx, dy in PLANE]
    peers += [to_z(z + d, k) for d in range(1, 16)]
    peers += [to_z(z + d, other) for d in RING]
    peers += [device(x, other, (y + d) % 4, zh, c) for d in range(4)]
    for peer in peers:
        pl.semaphore_signal(barrier, inc=1, device_id=peer, device_id_type=MESH)

    copy = Copies(send_sem, recv_sem)

    wf[...] = jnp.zeros_like(wf)
    wf[:, 0:160] = proj[pl.ds(pl.multiple_of(80 * (y % 2), 16), 80), :].astype(F32)
    pw[...] = pltpu.roll(wf[...], 32 * (c % 4), 1).astype(BF)

    pl.semaphore_wait(barrier, len(peers))

    def col_copy(n, to):
        return pltpu.make_async_remote_copy(
            src_ref=pw, dst_ref=zb.at[c % 4], send_sem=z_send.at[n], recv_sem=z_recv.at[c % 4],
            device_id=to, device_id_type=MESH)

    @pl.when(k == row_core)
    def _():
        for n, d in enumerate(NEAR):
            col_copy(n, to_z(z + d, col_core)).start()

        @pl.when(k != col_core)
        def _():
            col_copy(7, sibling).start()

        @pl.when(k == col_core)
        def _():
            zb[c % 4] = pw[...]

    tt[k] = tpl[...].T.reshape(4, 4, 80, 256)
    img_f = images[...].astype(F32)
    img[k] = (img_f * inv_norm(img_f)).astype(BF)
    lab[k] = labels[...]
    to_img = copy(img.at[k], img.at[k], sibling)
    to_lab = copy(lab.at[k], lab.at[k], sibling)
    to_tx = copy(tt.at[k], tt.at[k], sibling)

    for j in range(4):
        @pl.when(jnp.logical_or(4 * k + j != c, k != row_core))
        def _():
            pltpu.make_async_remote_copy(
                src_ref=pw, dst_ref=zb.at[j], send_sem=z_send.at[0], recv_sem=z_recv.at[j],
                device_id=sibling, device_id_type=MESH).wait_recv()

    @pl.when(k == row_core)
    def _():
        for n, d in enumerate(NEAR):
            col_copy(n, to_z(z + d, col_core)).wait_send()

        @pl.when(k != col_core)
        def _():
            col_copy(7, sibling).wait_send()
    tiles = [
        zb[0, :, 0:128],
        zb[0, :, 128:256] + zb[1, :, 0:128],
        zb[1, :, 128:256] + zb[2, :, 0:128],
        zb[2, :, 128:256] + zb[3, :, 0:128],
        zb[3, :, 128:256],
    ]
    for j, tile in enumerate(tiles):
        pf[k, x, y, :, j * 128:(j + 1) * 128] = tile

    def piece(d1, d2):
        px, py = place((first + d1) % 4, (second + d2) % 4)
        return pf.at[k, px, py]

    def send(d1, d2, to):
        return copy(piece(d1, d2), piece(d1, d2), to)

    shared = []
    ahead = {d: send(0, 0, to_first(d)) for d in (1, 3, 2)}
    up, down = {}, {}
    for d1 in (0, 3, 1, 2):
        if d1:
            ahead[(4 - d1) % 4].wait_recv()
        up[d1] = send(d1, 0, to_second(1))
        down[d1] = send(d1, 0, to_second(3))
        shared.append(send(d1, 0, sibling))
    far = {}
    for d1 in (0, 3, 1, 2):
        up[d1].wait_recv()
        if d1 in (0, 3):
            far[d1] = send(d1, 3, to_second(1))
        down[d1].wait_recv()
        if d1 in (1, 2):
            far[d1] = send(d1, 1, to_second(3))
        shared.append(send(d1, 3, sibling))
        shared.append(send(d1, 1, sibling))
    for d1 in (0, 1, 3, 2):
        far[d1].wait_recv()
        shared.append(send(d1, 2, sibling))
    for cp in shared:
        cp.wait_recv()

    for h in range(2):
        zbuf[:, h * 640:(h + 1) * 640] = jnp.dot(
            tpl[...], pf[h].reshape(1280, 640), preferred_element_type=F32)
    rz = inv_norm(zbuf[...])
    rzbuf[...] = rz
    zbuf[...] = zbuf[...] * rz
    total = zbuf[0:64] + zbuf[64:128] + zbuf[128:192] + zbuf[192:256]
    s_send[...] = total.astype(BF).reshape(4, 16, 1280)

    got = [copy(s_send.at[(y + d) % 4], s_recv.at[d - 1], to_plane(0, d)) for d in (2, 1, 3)]
    for cp in got:
        cp.wait_recv()
    own = s_send[y].astype(F32)
    for d in range(3):
        own = own + s_recv[d].astype(F32)
    c_send[...] = own.astype(BF)
    copy(c_send, c_recv, across).wait_recv()
    mbuf[x, y] = ((c_send[...].astype(F32) + c_recv[...].astype(F32)) / TPL).astype(BF)

    got = [copy(mbuf.at[x, y], mbuf.at[x, y], to_plane(dx, dy)) for dx, dy in PLANE]
    to_img.wait_recv()
    to_lab.wait_recv()
    to_tx.wait_recv()
    for cp in got:
        cp.wait_recv()

    mean = mbuf[...].reshape(256, 1280).astype(F32)
    cb[...] = (mean * inv_norm(mean)).astype(BF)
    for s in range(2):
        sc = lax.dot_general(cb[...], img[s], (((1,), (1,)), ((), ())), preferred_element_type=F32)
        ebuf[:, s * 256:(s + 1) * 256] = jnp.exp(SCALE * sc)
    e_send[...] = jnp.sum(ebuf[...], axis=0, keepdims=True)
    copy(e_send, e_one, sibling).wait_recv()
    e_two[...] = e_send[...] + e_one[...]
    got = [copy(e_two, e_recv.at[d - 1], device(x, k, y, zh, (c + d) % 8)) for d in range(1, 8)]
    row = lax.broadcasted_iota(jnp.int32, (256, 1), 0)
    ids = (c * 8 + (row // 64) * 2 + k) * 64 + row % 64
    for cp in got:
        cp.wait_recv()
    tot = e_two[...]
    for d in range(7):
        tot = tot + e_recv[d]
    inv = 1.0 / tot
    for s in range(2):
        part = slice(s * 256, (s + 1) * 256)
        hot = (lab[s, 0:1, :] == ids).astype(F32)
        gbuf[:, part] = (ebuf[:, part] * inv[:, part] - hot).astype(BF)

    def class_grad(n, _):
        o = pl.ds(pl.multiple_of(n * 256, 256), 256)
        v = jnp.dot(gbuf[...], img[:, :, o].reshape(512, 256), preferred_element_type=F32)
        cg_send[:, :, :, o] = (SCALE * v).astype(BF).reshape(4, 4, 16, 256)
        return 0
    lax.fori_loop(0, 5, class_grad, 0)

    got = []
    for n, (dx, dy) in enumerate(PLANE):
        px, py = at_plane(dx, dy)
        got.append(copy(cg_send.at[px, py], cg_recv.at[n], to_plane(dx, dy)))
    for cp in got:
        cp.wait_recv()
    own = cg_send[x, y].astype(F32)
    for n in range(15):
        own = own + cg_recv[n].astype(F32)
    f_send[...] = own.astype(BF)
    copy(f_send, f_recv, across).wait_recv()
    gs[y] = (f_send[...].astype(F32) + f_recv[...].astype(F32)).astype(BF)
    got = [copy(gs.at[y], gs.at[y], to_plane(0, d)) for d in (2, 1, 3)]
    mean = mbuf[x].reshape(64, 1280).astype(F32)
    rn = inv_norm(mean)
    class_w = mean * rn
    for cp in got:
        cp.wait_recv()

    class_g = gs[...].reshape(64, 1280).astype(F32)
    dot_wg = jnp.sum(class_w * class_g, axis=1, keepdims=True)
    per_u = (class_g - class_w * dot_wg) * rn / TPL
    for n in range(4):
        rows_n = slice(n * 64, (n + 1) * 64)
        u = zbuf[rows_n]
        inner = jnp.sum(u * per_u, axis=1, keepdims=True)
        gz[rows_n] = ((per_u - u * inner) * rzbuf[rows_n]).astype(BF)

    def half(core):
        return pl.ds(pl.multiple_of(640 * core, 128), 640)

    copy(gz.at[:, half(other)], gx, sibling).wait_recv()

    g_own, g_other = gz[:, half(k)], gx[...]
    got = {}
    for d in (2, 1, 3, 0):
        j = (first + d) % 4
        spots = [place(j, m) for m in range(4)]
        lhs = jnp.concatenate([tt[k, px, py] for px, py in spots], axis=0)
        v = jnp.dot(lhs, g_own, preferred_element_type=F32)
        lhs = jnp.concatenate([tt[other, px, py] for px, py in spots], axis=0)
        v = v + jnp.dot(lhs, g_other, preferred_element_type=F32)
        hs[j] = v.astype(BF).reshape(4, 80, 640)
        if d:
            got[d] = copy(hs.at[j], hr.at[d - 1], to_first(d))

    for m in range(4):
        v = 0.0
        for h in range(2):
            w = pf[h, m].reshape(320, 640)
            v = v + lax.dot_general(
                gz[:, h * 640:(h + 1) * 640], w, (((1,), (1,)), ((), ())), preferred_element_type=F32)
        gt_out[:, m * 320:(m + 1) * 320] = v.astype(BF)

    for d in (1, 3, 2):
        got[d].wait_recv()
    for m in range(4):
        own = hs[first, m].astype(F32)
        for d in range(3):
            own = own + hr[d, m].astype(F32)
        h2[m] = own.astype(BF)
    got = [copy(h2.at[(second + d) % 4], h2r.at[d - 1], to_second(d)) for d in (2, 1, 3)]
    for cp in got:
        cp.wait_recv()
    own = h2[second].astype(F32)
    for d in range(3):
        own = own + h2r[d].astype(F32)
    rs[...] = own.astype(BF)

    def block_copy(j):
        ahead = (4 * k + j - c + 8) % 8
        near = z + ahead - 8 * (ahead // 5)
        slot = (ahead + 6) % 7
        return ahead, pltpu.make_async_remote_copy(
            src_ref=rs.at[:, pl.ds(128 * j, 256)], dst_ref=w_recv.at[slot],
            send_sem=w_send.at[j], recv_sem=w_recv_sem.at[slot],
            device_id=to_z(near, k), device_id_type=MESH)

    for j in range(4):
        ahead_j, cp = block_copy(j)

        @pl.when(ahead_j != 0)
        def _():
            cp.start()

    def final_copy(n, core, py):
        return pltpu.make_async_remote_copy(
            src_ref=hp, dst_ref=hy.at[y % 2], send_sem=y_send.at[n], recv_sem=y_recv.at[y % 2],
            device_id=device(x, core, py, zh, c), device_id_type=MESH)

    @pl.when(k == col_core)
    def _():
        own = rs[:, pl.ds(pl.multiple_of(128 * (c % 4), 128), 256)].astype(F32)
        for n in range(7):
            pltpu.make_async_remote_copy(
                src_ref=h_send, dst_ref=w_recv.at[n], send_sem=w_send.at[0], recv_sem=w_recv_sem.at[n],
                device_id=sibling, device_id_type=MESH).wait_recv()
            own = own + w_recv[n].astype(F32)
        h_send[...] = own.astype(BF)
        cp = pltpu.make_async_remote_copy(
            src_ref=h_send, dst_ref=h_recv, send_sem=w_send.at[4], recv_sem=w_recv_sem.at[7],
            device_id=across, device_id_type=MESH)
        cp.start()
        cp.wait()
        whole = h_send[...].astype(F32) + h_recv[...].astype(F32)
        hp[...] = pltpu.roll(whole, (256 - 32 * (c % 4)) % 256, 1).astype(BF)
        for d in (2, 1, 3):
            final_copy(d, row_core, (y + d) % 4).start()

        @pl.when(k != row_core)
        def _():
            final_copy(0, row_core, y).start()

        @pl.when(k == row_core)
        def _():
            hy[y % 2] = hp[...]

    for n in range(2):
        @pl.when(jnp.logical_or(2 * k + n != y, k != col_core))
        def _():
            pltpu.make_async_remote_copy(
                src_ref=hp, dst_ref=hy.at[n], send_sem=y_send.at[0], recv_sem=y_recv.at[n],
                device_id=sibling, device_id_type=MESH).wait_recv()
        gp_out[80 * n:80 * n + 80] = hy[n, :, 0:160].astype(F32)

    for j in range(4):
        ahead_j, cp = block_copy(j)

        @pl.when(ahead_j != 0)
        def _():
            cp.wait_send()

    @pl.when(k == col_core)
    def _():
        for d in (2, 1, 3):
            final_copy(d, row_core, (y + d) % 4).wait_send()

        @pl.when(k != row_core)
        def _():
            final_copy(0, row_core, y).wait_send()
    copy.finish()


def body(images, labels, templates, projection):
    flat = templates.reshape(256, 1280)
    lab = jnp.broadcast_to(labels.reshape(1, 256), (8, 256))
    vm = pl.BlockSpec(memory_space=pltpu.VMEM)
    scratch = [
        ((80, 256), F32), ((80, 256), BF), ((4, 80, 256), BF), ((2, 4, 4, 80, 640), BF),
        ((2, 4, 4, 80, 256), BF), ((256, 1280), F32), ((256, 1), F32),
        ((4, 16, 1280), BF), ((3, 16, 1280), BF), ((16, 1280), BF), ((16, 1280), BF),
        ((4, 4, 16, 1280), BF), ((256, 1280), BF), ((2, 256, 1280), BF), ((2, 8, 256), jnp.int32),
        ((256, 512), F32), ((1, 512), F32), ((1, 512), F32), ((1, 512), F32), ((7, 1, 512), F32),
        ((256, 512), BF), ((4, 4, 16, 1280), BF), ((15, 16, 1280), BF), ((16, 1280), BF), ((16, 1280), BF),
        ((4, 16, 1280), BF), ((256, 1280), BF), ((256, 640), BF),
        ((4, 4, 80, 640), BF), ((3, 4, 80, 640), BF), ((4, 80, 640), BF), ((3, 80, 640), BF),
        ((80, 640), BF), ((7, 80, 256), BF), ((80, 256), BF), ((80, 256), BF), ((80, 256), BF),
        ((2, 80, 256), BF),
    ]
    sems = (N_COPIES, N_COPIES, 8, 4, 5, 8, 4, 2)
    gt, gp = pl.pallas_call(
        kernel,
        out_shape=(jax.ShapeDtypeStruct((256, 1280), BF), jax.ShapeDtypeStruct((160, 160), F32)),
        in_specs=[vm] * 4,
        out_specs=(vm, vm),
        scratch_shapes=[pltpu.VMEM(s, d) for s, d in scratch]
        + [pltpu.SemaphoreType.DMA((n,)) for n in sems],
        compiler_params=pltpu.CompilerParams(
            collective_id=0, has_side_effects=True, vmem_limit_bytes=50 << 20),
    )(images, lab, flat, projection)
    return gt.reshape(templates.shape), gp


def solution(mesh):
    in_specs = (
        P(("img", "tpl"), None),
        P(("img", "tpl")),
        P("tpl", ("cls", "img"), None),
        P("img", "cls"),
    )
    out_specs = (P("tpl", ("cls", "img"), None), P("img", "cls"))
    return jax.shard_map(body, mesh=mesh, in_specs=in_specs, out_specs=out_specs, check_vma=False)
```

```python
import jax
import jax.numpy as jnp
from jax import lax
from jax.experimental import pallas as pl
from jax.experimental.pallas import tpu as pltpu
from jax.sharding import PartitionSpec as P

SCALE = 50.0
EPS = 1e-06
TPL = 32
MESH = pl.DeviceIdType.MESH
BF = jnp.bfloat16
F32 = jnp.float32
PLANE = [(a, b) for a in range(4) for b in range(4) if (a, b) != (0, 0)]
RING = (4, -4, 3, -3, 2, -2, 1, -1)


def inv_norm(v):
    return lax.rsqrt(jnp.sum(v * v, axis=-1, keepdims=True) + EPS)


def device(x, k, y, zh, zl):
    return (x * 2 + k, zl, zh * 4 + y)


class Copies:
    def __init__(self, send, recv):
        self.send, self.recv, self.used = send, recv, 0
        self.open = []

    def __call__(self, src, dst, to):
        n = self.used
        self.used += 1
        cp = pltpu.make_async_remote_copy(
            src_ref=src, dst_ref=dst, send_sem=self.send.at[n], recv_sem=self.recv.at[n],
            device_id=to, device_id_type=MESH)
        cp.start()
        self.open.append(cp)
        return cp

    def finish(self):
        for cp in self.open:
            cp.wait_send()


N_COPIES = 190
NEAR = (4, 3, -3, 2, -2, 1, -1)


def kernel(images_in, labels_in, tpl_in, proj_in, gt_out, gp_out,
           images, tpl, proj, wf, pw, zb, pf, tt, zbuf, rzbuf, s_send, s_recv, c_send, c_recv, mbuf, mo, cb,
           img, lab, ebuf, e_send, e_recv, gbuf, cg_send, cg_recv, f2, f2r, f_send, f_recv, gs, gz, gx,
           hs, hr, h2, h2r, rs, w_recv, h_send, h_recv, hp, hy,
           load_sem, send_sem, recv_sem, z_send, z_recv, w_send, w_recv_sem, y_send, y_recv):
    i = lax.axis_index("img")
    c = lax.axis_index("cls")
    t = lax.axis_index("tpl")
    x, k, y, zh = i // 2, i % 2, t % 4, t // 4
    z = zh * 8 + c
    other = 1 - k
    row_core, col_core = y // 2, c // 4

    def at_plane(dx, dy):
        return (x + dx) % 4, (y + dy) % 4

    def to_plane(dx, dy):
        px, py = at_plane(dx, dy)
        return device(px, k, py, zh, c)

    def to_z(n, core):
        n = (n + 16) % 16
        return device(x, core, y, n // 8, n % 8)

    def to_first(d):
        return device((x + d * other) % 4, k, (y + d * k) % 4, zh, c)

    def to_second(d):
        return device((x + d * k) % 4, k, (y + d * other) % 4, zh, c)

    def place(first, second):
        return first * other + second * k, second * other + first * k

    first, second = place(x, y)
    sibling = device(x, other, y, zh, c)
    across = device(x, k, y, 1 - zh, c)

    barrier = pltpu.get_barrier_semaphore()
    peers = [to_plane(dx, dy) for dx, dy in PLANE]
    peers += [to_z(z + d, k) for d in RING]
    peers += [to_z(z + d, other) for d in RING]
    peers += [device(x, other, (y + d) % 4, zh, c) for d in range(4)]
    for peer in peers:
        pl.semaphore_signal(barrier, inc=1, device_id=peer, device_id_type=MESH)

    loads = [
        pltpu.make_async_copy(src, dst, load_sem.at[n])
        for n, (src, dst) in enumerate(
            ((proj_in, proj), (tpl_in, tpl), (images_in, images), (labels_in, lab.at[k])))
    ]
    for load in loads:
        load.start()

    copy = Copies(send_sem, recv_sem)

    wf[...] = jnp.zeros_like(wf)
    loads[0].wait()
    wf[:, 0:160] = proj[pl.ds(pl.multiple_of(80 * (y % 2), 16), 80), :].astype(F32)
    pw[...] = pltpu.roll(wf[...], 32 * (c % 4), 1).astype(BF)

    pl.semaphore_wait(barrier, len(peers))

    def col_copy(n, to):
        return pltpu.make_async_remote_copy(
            src_ref=pw, dst_ref=zb.at[c % 4], send_sem=z_send.at[n], recv_sem=z_recv.at[c % 4],
            device_id=to, device_id_type=MESH)

    @pl.when(k == row_core)
    def _():
        for n, d in enumerate(NEAR):
            col_copy(n, to_z(z + d, col_core)).start()

        @pl.when(k != col_core)
        def _():
            col_copy(7, sibling).start()

        @pl.when(k == col_core)
        def _():
            zb[c % 4] = pw[...]

    for load in loads[1:]:
        load.wait()
    tt[k] = tpl[...].T.reshape(4, 4, 80, 256)
    img_f = images[...].astype(F32)
    img[k] = (img_f * inv_norm(img_f)).astype(BF)
    to_img = copy(img.at[k], img.at[k], sibling)
    to_lab = copy(lab.at[k], lab.at[k], sibling)
    to_tx = copy(tt.at[k], tt.at[k], sibling)

    for j in range(4):
        @pl.when(jnp.logical_or(4 * k + j != c, k != row_core))
        def _():
            pltpu.make_async_remote_copy(
                src_ref=pw, dst_ref=zb.at[j], send_sem=z_send.at[0], recv_sem=z_recv.at[j],
                device_id=sibling, device_id_type=MESH).wait_recv()

    @pl.when(k == row_core)
    def _():
        for n, d in enumerate(NEAR):
            col_copy(n, to_z(z + d, col_core)).wait_send()

        @pl.when(k != col_core)
        def _():
            col_copy(7, sibling).wait_send()
    tiles = [
        zb[0, :, 0:128],
        zb[0, :, 128:256] + zb[1, :, 0:128],
        zb[1, :, 128:256] + zb[2, :, 0:128],
        zb[2, :, 128:256] + zb[3, :, 0:128],
        zb[3, :, 128:256],
    ]
    for j, tile in enumerate(tiles):
        pf[k, x, y, :, j * 128:(j + 1) * 128] = tile

    def piece(d1, d2):
        px, py = place((first + d1) % 4, (second + d2) % 4)
        return pf.at[k, px, py]

    def send(d1, d2, to):
        return copy(piece(d1, d2), piece(d1, d2), to)

    shared = []
    ahead = {d: send(0, 0, to_first(d)) for d in (1, 3, 2)}
    up, down = {}, {}
    for d1 in (0, 3, 1, 2):
        if d1:
            ahead[(4 - d1) % 4].wait_recv()
        up[d1] = send(d1, 0, to_second(1))
        down[d1] = send(d1, 0, to_second(3))
        shared.append(send(d1, 0, sibling))
    far = {}
    for d1 in (0, 3, 1, 2):
        up[d1].wait_recv()
        if d1 in (0, 3):
            far[d1] = send(d1, 3, to_second(1))
        down[d1].wait_recv()
        if d1 in (1, 2):
            far[d1] = send(d1, 1, to_second(3))
        shared.append(send(d1, 3, sibling))
        shared.append(send(d1, 1, sibling))
    for d1 in (0, 1, 3, 2):
        far[d1].wait_recv()
        shared.append(send(d1, 2, sibling))
    for cp in shared:
        cp.wait_recv()

    for h in range(2):
        zbuf[:, h * 640:(h + 1) * 640] = jnp.dot(
            tpl[...], pf[h].reshape(1280, 640), preferred_element_type=F32)
    rz = inv_norm(zbuf[...])
    rzbuf[...] = rz
    zbuf[...] = zbuf[...] * rz
    total = zbuf[0:64] + zbuf[64:128] + zbuf[128:192] + zbuf[192:256]
    s_send[...] = total.astype(BF).reshape(4, 16, 1280)

    halves = [pl.ds(0, 640), pl.ds(640, 640)]
    got = [
        [copy(s_send.at[(y + d) % 4, :, h], s_recv.at[d - 1, :, h], to_plane(0, d)) for d in (2, 1, 3)]
        for h in halves
    ]
    four = []
    for n, h in enumerate(halves):
        for cp in got[n]:
            cp.wait_recv()
        own = s_send[y, :, h].astype(F32)
        for d in range(3):
            own = own + s_recv[d, :, h].astype(F32)
        c_send[:, h] = own.astype(BF)
        four.append([
            copy(c_send.at[:, h], c_recv.at[0, :, h], to_z(z + 4, k)),
            copy(c_send.at[:, h], c_recv.at[1, :, h], to_z(z - 4, k))])

    def mean_piece(d1, h):
        px, py = place((first + d1) % 4, second)
        return mbuf.at[px, py, :, h]

    ahead, wide, back = [], [], []
    for n, h in enumerate(halves):
        for cp in four[n]:
            cp.wait_recv()
        mbuf[x, y, :, h] = ((c_recv[0, :, h].astype(F32) + c_recv[1, :, h].astype(F32)) / TPL).astype(BF)
        src = mean_piece(0, h)
        ahead.append({d: copy(src, src, to_first(d)) for d in (2, 1, 3)})
        wide += [copy(src, src, to_second(d)) for d in (2, 1, 3)]
        back.append(copy(src, mo.at[:, h], to_z(z + 4 - 8 * n, k)))
    for n, h in enumerate(halves):
        for d in (3, 1, 2):
            ahead[n][d].wait_recv()
            src = mean_piece(4 - d, h)
            wide += [copy(src, src, to_second(e)) for e in (2, 1, 3)]
    to_img.wait_recv()
    to_lab.wait_recv()
    to_tx.wait_recv()
    for cp in wide:
        cp.wait_recv()
    mean = mbuf[...].reshape(256, 1280).astype(F32)
    cb[...] = (mean * inv_norm(mean)).astype(BF)
    for s in range(2):
        sc = lax.dot_general(cb[...], img[s], (((1,), (1,)), ((), ())), preferred_element_type=F32)
        ebuf[:, s * 256:(s + 1) * 256] = jnp.exp(SCALE * sc)
    e_send[...] = jnp.sum(ebuf[...], axis=0, keepdims=True)
    got = []
    for d in (4, 3, 5, 2, 6, 1, 7):
        for core in (k, other):
            got.append(copy(e_send, e_recv.at[len(got)], device(x, core, y, zh, (c + d) % 8)))
    got.append(copy(e_send, e_recv.at[14], sibling))
    row = lax.broadcasted_iota(jnp.int32, (256, 1), 0)
    ids = (((c + 4) % 8) * 8 + (row // 64) * 2 + k) * 64 + row % 64
    for cp in got:
        cp.wait_recv()
    tot = e_send[...]
    for n in range(15):
        tot = tot + e_recv[n]
    inv = 1.0 / tot
    for s in range(2):
        part = slice(s * 256, (s + 1) * 256)
        hot = (lab[s, 0:1, :] == ids).astype(F32)
        gbuf[:, part] = (ebuf[:, part] * inv[:, part] - hot).astype(BF)

    got = []
    for n, h in enumerate(halves):
        v = jnp.dot(gbuf[...], img[:, :, h].reshape(512, 640), preferred_element_type=F32)
        cg_send[n] = (SCALE * v).astype(BF).reshape(4, 4, 16, 640)
        got.append([])
        for d in (2, 1, 3):
            for m in range(4):
                px, py = place((first + d) % 4, m)
                got[n].append(copy(cg_send.at[n, px, py], cg_recv.at[n, d - 1, m], to_first(d)))
    step = []
    for n in range(2):
        for cp in got[n]:
            cp.wait_recv()
        for m in range(4):
            px, py = place(first, m)
            own = cg_send[n, px, py].astype(F32)
            for d in range(3):
                own = own + cg_recv[n, d, m].astype(F32)
            f2[n, m] = own.astype(BF)
        step.append([
            copy(f2.at[n, (second + d) % 4], f2r.at[n, d - 1], to_second(d)) for d in (2, 1, 3)])
    four = []
    for n, h in enumerate(halves):
        for cp in step[n]:
            cp.wait_recv()
        own = f2[n, second].astype(F32)
        for d in range(3):
            own = own + f2r[n, d].astype(F32)
        f_send[:, h] = own.astype(BF)
        four += [
            copy(f_send.at[:, h], f_recv.at[0, :, h], to_z(z + 4, k)),
            copy(f_send.at[:, h], f_recv.at[1, :, h], to_z(z - 4, k))]
    for cp in back:
        cp.wait_recv()
    mean = mo[...].astype(F32)
    rn = inv_norm(mean)
    class_w = mean * rn
    for cp in four:
        cp.wait_recv()
    class_g = f_recv[0].astype(F32) + f_recv[1].astype(F32)
    dot_wg = jnp.sum(class_w * class_g, axis=1, keepdims=True)
    gs[y] = ((class_g - class_w * dot_wg) * rn / TPL).astype(BF)
    for cp in [copy(gs.at[y], gs.at[y], to_plane(0, d)) for d in (2, 1, 3)]:
        cp.wait_recv()
    per_u = gs[...].reshape(64, 1280).astype(F32)
    for n in range(4):
        rows_n = slice(n * 64, (n + 1) * 64)
        u = zbuf[rows_n]
        inner = jnp.sum(u * per_u, axis=1, keepdims=True)
        gz[rows_n] = ((per_u - u * inner) * rzbuf[rows_n]).astype(BF)

    def half(core):
        return pl.ds(pl.multiple_of(640 * core, 128), 640)

    copy(gz.at[:, half(other)], gx, sibling).wait_recv()

    g_own, g_other = gz[:, half(k)], gx[...]
    got = {}
    for d in (2, 1, 3, 0):
        j = (first + d) % 4
        spots = [place(j, m) for m in range(4)]
        lhs = jnp.concatenate([tt[k, px, py] for px, py in spots], axis=0)
        v = jnp.dot(lhs, g_own, preferred_element_type=F32)
        lhs = jnp.concatenate([tt[other, px, py] for px, py in spots], axis=0)
        v = v + jnp.dot(lhs, g_other, preferred_element_type=F32)
        hs[j] = v.astype(BF).reshape(4, 80, 640)
        if d:
            got[d] = copy(hs.at[j], hr.at[d - 1], to_first(d))

    for m in range(4):
        v = 0.0
        for h in range(2):
            w = pf[h, m].reshape(320, 640)
            v = v + lax.dot_general(
                gz[:, h * 640:(h + 1) * 640], w, (((1,), (1,)), ((), ())), preferred_element_type=F32)
        gt_out[:, m * 320:(m + 1) * 320] = v.astype(BF)

    for d in (1, 3, 2):
        got[d].wait_recv()
    for m in range(4):
        own = hs[first, m].astype(F32)
        for d in range(3):
            own = own + hr[d, m].astype(F32)
        h2[m] = own.astype(BF)
    got = [copy(h2.at[(second + d) % 4], h2r.at[d - 1], to_second(d)) for d in (2, 1, 3)]
    for cp in got:
        cp.wait_recv()
    own = h2[second].astype(F32)
    for d in range(3):
        own = own + h2r[d].astype(F32)
    rs[...] = own.astype(BF)

    def block_copy(j):
        ahead = (4 * k + j - c + 8) % 8
        near = z + ahead - 8 * (ahead // 5)
        slot = (ahead + 6) % 7
        return ahead, pltpu.make_async_remote_copy(
            src_ref=rs.at[:, pl.ds(128 * j, 256)], dst_ref=w_recv.at[slot],
            send_sem=w_send.at[j], recv_sem=w_recv_sem.at[slot],
            device_id=to_z(near, k), device_id_type=MESH)

    for j in range(4):
        ahead_j, cp = block_copy(j)

        @pl.when(ahead_j != 0)
        def _():
            cp.start()

    def final_copy(n, core, py):
        return pltpu.make_async_remote_copy(
            src_ref=hp, dst_ref=hy.at[y % 2], send_sem=y_send.at[n], recv_sem=y_recv.at[y % 2],
            device_id=device(x, core, py, zh, c), device_id_type=MESH)

    @pl.when(k == col_core)
    def _():
        own = rs[:, pl.ds(pl.multiple_of(128 * (c % 4), 128), 256)].astype(F32)
        for n in range(7):
            pltpu.make_async_remote_copy(
                src_ref=h_send, dst_ref=w_recv.at[n], send_sem=w_send.at[0], recv_sem=w_recv_sem.at[n],
                device_id=sibling, device_id_type=MESH).wait_recv()
            own = own + w_recv[n].astype(F32)
        h_send[...] = own.astype(BF)
        cp = pltpu.make_async_remote_copy(
            src_ref=h_send, dst_ref=h_recv, send_sem=w_send.at[4], recv_sem=w_recv_sem.at[7],
            device_id=across, device_id_type=MESH)
        cp.start()
        cp.wait()
        whole = h_send[...].astype(F32) + h_recv[...].astype(F32)
        hp[...] = pltpu.roll(whole, (256 - 32 * (c % 4)) % 256, 1).astype(BF)
        for d in (2, 1, 3):
            final_copy(d, row_core, (y + d) % 4).start()

        @pl.when(k != row_core)
        def _():
            final_copy(0, row_core, y).start()

        @pl.when(k == row_core)
        def _():
            hy[y % 2] = hp[...]

    for n in range(2):
        @pl.when(jnp.logical_or(2 * k + n != y, k != col_core))
        def _():
            pltpu.make_async_remote_copy(
                src_ref=hp, dst_ref=hy.at[n], send_sem=y_send.at[0], recv_sem=y_recv.at[n],
                device_id=sibling, device_id_type=MESH).wait_recv()
        gp_out[80 * n:80 * n + 80] = hy[n, :, 0:160].astype(F32)

    for j in range(4):
        ahead_j, cp = block_copy(j)

        @pl.when(ahead_j != 0)
        def _():
            cp.wait_send()

    @pl.when(k == col_core)
    def _():
        for d in (2, 1, 3):
            final_copy(d, row_core, (y + d) % 4).wait_send()

        @pl.when(k != row_core)
        def _():
            final_copy(0, row_core, y).wait_send()
    copy.finish()


def body(images, labels, templates, projection):
    flat = templates.reshape(256, 1280)
    vm = pl.BlockSpec(memory_space=pltpu.VMEM)
    hbm = pl.BlockSpec(memory_space=pl.ANY)
    scratch = [
        ((256, 1280), BF), ((256, 1280), BF), ((160, 160), BF),
        ((80, 256), F32), ((80, 256), BF), ((4, 80, 256), BF), ((2, 4, 4, 80, 640), BF),
        ((2, 4, 4, 80, 256), BF), ((256, 1280), F32), ((256, 1), F32),
        ((4, 16, 1280), BF), ((3, 16, 1280), BF), ((16, 1280), BF), ((2, 16, 1280), BF),
        ((4, 4, 16, 1280), BF), ((16, 1280), BF), ((256, 1280), BF), ((2, 256, 1280), BF),
        ((2, 1, 256), jnp.int32), ((256, 512), F32), ((1, 512), F32), ((15, 1, 512), F32),
        ((256, 512), BF), ((2, 4, 4, 16, 640), BF), ((2, 3, 4, 16, 640), BF), ((2, 4, 16, 640), BF),
        ((2, 3, 16, 640), BF), ((16, 1280), BF), ((2, 16, 1280), BF),
        ((4, 16, 1280), BF), ((256, 1280), BF), ((256, 640), BF),
        ((4, 4, 80, 640), BF), ((3, 4, 80, 640), BF), ((4, 80, 640), BF), ((3, 80, 640), BF),
        ((80, 640), BF), ((7, 80, 256), BF), ((80, 256), BF), ((80, 256), BF), ((80, 256), BF),
        ((2, 80, 256), BF),
    ]
    sems = (4, N_COPIES, N_COPIES, 8, 4, 5, 8, 4, 2)
    gt, gp = pl.pallas_call(
        kernel,
        out_shape=(jax.ShapeDtypeStruct((256, 1280), BF), jax.ShapeDtypeStruct((160, 160), F32)),
        in_specs=[hbm] * 4,
        out_specs=(vm, vm),
        scratch_shapes=[pltpu.VMEM(s, d) for s, d in scratch]
        + [pltpu.SemaphoreType.DMA((n,)) for n in sems],
        compiler_params=pltpu.CompilerParams(
            collective_id=0, has_side_effects=True, vmem_limit_bytes=60 << 20),
    )(images, labels.reshape(1, 256), flat, projection)
    return gt.reshape(templates.shape), gp


def solution(mesh):
    in_specs = (
        P(("img", "tpl"), None),
        P(("img", "tpl")),
        P("tpl", ("cls", "img"), None),
        P("img", "cls"),
    )
    out_specs = (P("tpl", ("cls", "img"), None), P("img", "cls"))
    return jax.shard_map(body, mesh=mesh, in_specs=in_specs, out_specs=out_specs, check_vma=False)
```

```python
import jax
import jax.numpy as jnp
from jax import lax
from jax.experimental import pallas as pl
from jax.experimental.pallas import tpu as pltpu
from jax.sharding import PartitionSpec as P

SCALE = 50.0
EPS = 1e-06
TPL = 32
MESH = pl.DeviceIdType.MESH
BF = jnp.bfloat16
F32 = jnp.float32
PLANE = [(a, b) for a in range(4) for b in range(4) if (a, b) != (0, 0)]
RING = (4, -4, 3, -3, 2, -2, 1, -1)


def inv_norm(v):
    return lax.rsqrt(jnp.sum(v * v, axis=-1, keepdims=True) + EPS)


def device(x, k, y, zh, zl):
    return (x * 2 + k, zl, zh * 4 + y)


class Copies:
    def __init__(self, send, recv):
        self.send, self.recv, self.used = send, recv, 0
        self.open = []

    def __call__(self, src, dst, to):
        n = self.used
        self.used += 1
        cp = pltpu.make_async_remote_copy(
            src_ref=src, dst_ref=dst, send_sem=self.send.at[n], recv_sem=self.recv.at[n],
            device_id=to, device_id_type=MESH)
        cp.start()
        self.open.append(cp)
        return cp

    def finish(self):
        for cp in self.open:
            cp.wait_send()


N_COPIES = 190


def kernel(images_in, labels_in, tpl_in, proj_in, gt_low, gt_high, gp_out,
           gt_out, images, tpl, proj, wf, pw, zb, pf, tt, zbuf, rzbuf, s_send, s_recv, c_send, c_recv, mbuf, mo, cb,
           img, lab, ebuf, e_send, e_recv, gbuf, cg_send, cg_recv, f2, f2r, f_send, f_recv, gs, gz, gx,
           hs, hr, hc, h2, h2r, rs, w_recv, h_send, h_recv, hp, hy,
           load_sem, store_sem, send_sem, recv_sem, z_send, z_recv, w_send, w_recv_sem, y_send, y_recv):
    i = lax.axis_index("img")
    c = lax.axis_index("cls")
    t = lax.axis_index("tpl")
    x, k, y, zh = i // 2, i % 2, t % 4, t // 4
    z = zh * 8 + c
    other = 1 - k
    row_core, col_core = y // 2, c // 4

    def at_plane(dx, dy):
        return (x + dx) % 4, (y + dy) % 4

    def to_plane(dx, dy):
        px, py = at_plane(dx, dy)
        return device(px, k, py, zh, c)

    def to_z(n, core):
        n = (n + 16) % 16
        return device(x, core, y, n // 8, n % 8)

    def to_first(d):
        return device((x + d * other) % 4, k, (y + d * k) % 4, zh, c)

    def to_second(d):
        return device((x + d * k) % 4, k, (y + d * other) % 4, zh, c)

    def place(first, second):
        return first * other + second * k, second * other + first * k

    first, second = place(x, y)
    sibling = device(x, other, y, zh, c)

    barrier = pltpu.get_barrier_semaphore()
    peers = [to_plane(dx, dy) for dx, dy in PLANE]
    peers += [to_z(z + d, k) for d in RING]
    peers += [to_z(z + d, other) for d in RING]
    peers += [device(x, other, (y + d) % 4, zh, c) for d in range(4)]
    for peer in peers:
        pl.semaphore_signal(barrier, inc=1, device_id=peer, device_id_type=MESH)

    loads = [
        pltpu.make_async_copy(src, dst, load_sem.at[n])
        for n, (src, dst) in enumerate(
            ((proj_in, proj), (tpl_in, tpl), (images_in, images), (labels_in, lab.at[k])))
    ]
    for load in loads:
        load.start()

    copy = Copies(send_sem, recv_sem)

    wf[...] = jnp.zeros_like(wf)
    loads[0].wait()
    wf[:, 0:160] = proj[pl.ds(pl.multiple_of(80 * (y % 2), 16), 80), :].astype(F32)
    pw[...] = pltpu.roll(wf[...], 32 * (c % 4), 1).astype(BF)

    pl.semaphore_wait(barrier, len(peers))

    def col_copy(n, d, to, slot=None):
        rows = pl.ds(0, 48) if d == 4 else pl.ds(48, 32) if d == -4 else pl.ds(0, 80)
        slot = c % 4 if slot is None else slot
        return pltpu.make_async_remote_copy(
            src_ref=pw.at[rows], dst_ref=zb.at[slot, rows], send_sem=z_send.at[n],
            recv_sem=z_recv.at[4 if d == -4 else slot], device_id=to, device_id_type=MESH)

    @pl.when(k == row_core)
    def _():
        for n, d in enumerate(RING):
            col_copy(n, d, to_z(z + d, col_core)).start()

        @pl.when(k != col_core)
        def _():
            col_copy(8, 0, sibling).start()

        @pl.when(k == col_core)
        def _():
            zb[c % 4] = pw[...]

    for load in loads[1:]:
        load.wait()
    tt[k] = tpl[...].T.reshape(4, 4, 80, 256)
    img_f = images[...].astype(F32)
    img[k] = (img_f * inv_norm(img_f)).astype(BF)
    to_img = copy(img.at[k], img.at[k], sibling)
    to_lab = copy(lab.at[k], lab.at[k], sibling)
    to_tx = copy(tt.at[k], tt.at[k], sibling)

    for j in range(4):
        block = 4 * k + j

        @pl.when(block == (c + 4) % 8)
        def _():
            col_copy(0, 4, sibling, j).wait_recv()
            col_copy(0, -4, sibling, j).wait_recv()

        @pl.when(jnp.logical_and(block != (c + 4) % 8, jnp.logical_or(block != c, k != row_core)))
        def _():
            col_copy(0, 0, sibling, j).wait_recv()

    @pl.when(k == row_core)
    def _():
        for n, d in enumerate(RING):
            col_copy(n, d, to_z(z + d, col_core)).wait_send()

        @pl.when(k != col_core)
        def _():
            col_copy(8, 0, sibling).wait_send()
    tiles = [
        zb[0, :, 0:128],
        zb[0, :, 128:256] + zb[1, :, 0:128],
        zb[1, :, 128:256] + zb[2, :, 0:128],
        zb[2, :, 128:256] + zb[3, :, 0:128],
        zb[3, :, 128:256],
    ]
    for j, tile in enumerate(tiles):
        pf[k, x, y, :, j * 128:(j + 1) * 128] = tile

    def piece(d1, d2):
        px, py = place((first + d1) % 4, (second + d2) % 4)
        return pf.at[k, px, py]

    def send(d1, d2, to):
        return copy(piece(d1, d2), piece(d1, d2), to)

    shared = []
    ahead = {d: send(0, 0, to_first(d)) for d in (1, 3, 2)}
    up, down = {}, {}
    for d1 in (0, 3, 1, 2):
        if d1:
            ahead[(4 - d1) % 4].wait_recv()
        up[d1] = send(d1, 0, to_second(1))
        down[d1] = send(d1, 0, to_second(3))
        shared.append(send(d1, 0, sibling))
    far = {}
    for d1 in (0, 3, 1, 2):
        up[d1].wait_recv()
        if d1 in (0, 3):
            far[d1] = send(d1, 3, to_second(1))
        down[d1].wait_recv()
        if d1 in (1, 2):
            far[d1] = send(d1, 1, to_second(3))
        shared.append(send(d1, 3, sibling))
        shared.append(send(d1, 1, sibling))
    for d1 in (0, 1, 3, 2):
        far[d1].wait_recv()
        shared.append(send(d1, 2, sibling))

    def half(core):
        return pl.ds(pl.multiple_of(640 * core, 128), 640)

    def project(core):
        zbuf[:, half(core)] = jnp.dot(tpl[...], pf[core].reshape(1280, 640), preferred_element_type=F32)

    project(k)
    for cp in shared:
        cp.wait_recv()
    project(other)
    rz = inv_norm(zbuf[...])
    rzbuf[...] = rz
    zbuf[...] = zbuf[...] * rz
    total = zbuf[0:64] + zbuf[64:128] + zbuf[128:192] + zbuf[192:256]
    s_send[...] = total.astype(BF).reshape(4, 16, 1280)

    halves = [pl.ds(0, 640), pl.ds(640, 640)]
    got = [
        [copy(s_send.at[(y + d) % 4, :, h], s_recv.at[d - 1, :, h], to_plane(0, d)) for d in (2, 1, 3)]
        for h in halves
    ]
    four = []
    for n, h in enumerate(halves):
        for cp in got[n]:
            cp.wait_recv()
        own = s_send[y, :, h].astype(F32)
        for d in range(3):
            own = own + s_recv[d, :, h].astype(F32)
        c_send[:, h] = own.astype(BF)
        four.append([
            copy(c_send.at[:, h], c_recv.at[0, :, h], to_z(z + 4, k)),
            copy(c_send.at[:, h], c_recv.at[1, :, h], to_z(z - 4, k))])

    def mean_piece(d1, h):
        px, py = place((first + d1) % 4, second)
        return mbuf.at[px, py, :, h]

    ahead, wide, back = [], [], []
    for n, h in enumerate(halves):
        for cp in four[n]:
            cp.wait_recv()
        mbuf[x, y, :, h] = ((c_recv[0, :, h].astype(F32) + c_recv[1, :, h].astype(F32)) / TPL).astype(BF)
        src = mean_piece(0, h)
        ahead.append({d: copy(src, src, to_first(d)) for d in (2, 1, 3)})
        wide += [copy(src, src, to_second(d)) for d in (2, 1, 3)]
        back.append(copy(src, mo.at[:, h], to_z(z + 4 - 8 * n, k)))
    for n, h in enumerate(halves):
        for d in (3, 1, 2):
            ahead[n][d].wait_recv()
            src = mean_piece(4 - d, h)
            wide += [copy(src, src, to_second(e)) for e in (2, 1, 3)]
    to_img.wait_recv()
    to_lab.wait_recv()
    to_tx.wait_recv()
    for cp in wide:
        cp.wait_recv()
    mean = mbuf[...].reshape(256, 1280).astype(F32)
    cb[...] = (mean * inv_norm(mean)).astype(BF)
    for s in range(2):
        sc = lax.dot_general(cb[...], img[s], (((1,), (1,)), ((), ())), preferred_element_type=F32)
        ebuf[:, s * 256:(s + 1) * 256] = jnp.exp(SCALE * sc)
    e_send[...] = jnp.sum(ebuf[...], axis=0, keepdims=True)
    got = []
    for d in (4, 3, 5, 2, 6, 1, 7):
        for core in (k, other):
            got.append(copy(e_send, e_recv.at[len(got)], device(x, core, y, zh, (c + d) % 8)))
    got.append(copy(e_send, e_recv.at[14], sibling))
    row = lax.broadcasted_iota(jnp.int32, (256, 1), 0)
    ids = (((c + 4) % 8) * 8 + (row // 64) * 2 + k) * 64 + row % 64
    for cp in got:
        cp.wait_recv()
    tot = e_send[...]
    for n in range(15):
        tot = tot + e_recv[n]
    inv = 1.0 / tot
    for s in range(2):
        part = slice(s * 256, (s + 1) * 256)
        hot = (lab[s, 0:1, :] == ids).astype(F32)
        gbuf[:, part] = (ebuf[:, part] * inv[:, part] - hot).astype(BF)

    got = []
    for n, h in enumerate(halves):
        v = jnp.dot(gbuf[...], img[:, :, h].reshape(512, 640), preferred_element_type=F32)
        cg_send[n] = (SCALE * v).astype(BF).reshape(4, 4, 16, 640)
        got.append([])
        for d in (2, 1, 3):
            for m in range(4):
                px, py = place((first + d) % 4, m)
                got[n].append(copy(cg_send.at[n, px, py], cg_recv.at[n, d - 1, m], to_first(d)))
    step = []
    for n in range(2):
        for cp in got[n]:
            cp.wait_recv()
        for m in range(4):
            px, py = place(first, m)
            own = cg_send[n, px, py].astype(F32)
            for d in range(3):
                own = own + cg_recv[n, d, m].astype(F32)
            f2[n, m] = own.astype(BF)
        step.append([
            copy(f2.at[n, (second + d) % 4], f2r.at[n, d - 1], to_second(d)) for d in (2, 1, 3)])
    four = []
    for n, h in enumerate(halves):
        for cp in step[n]:
            cp.wait_recv()
        own = f2[n, second].astype(F32)
        for d in range(3):
            own = own + f2r[n, d].astype(F32)
        f_send[:, h] = own.astype(BF)
        four += [
            copy(f_send.at[:, h], f_recv.at[0, :, h], to_z(z + 4, k)),
            copy(f_send.at[:, h], f_recv.at[1, :, h], to_z(z - 4, k))]
    for cp in back:
        cp.wait_recv()
    mean = mo[...].astype(F32)
    rn = inv_norm(mean)
    class_w = mean * rn
    for cp in four:
        cp.wait_recv()
    class_g = f_recv[0].astype(F32) + f_recv[1].astype(F32)
    dot_wg = jnp.sum(class_w * class_g, axis=1, keepdims=True)
    gs[y] = ((class_g - class_w * dot_wg) * rn / TPL).astype(BF)
    for cp in [copy(gs.at[y], gs.at[y], to_plane(0, d)) for d in (2, 1, 3)]:
        cp.wait_recv()
    per_u = gs[...].reshape(64, 1280).astype(F32)
    for n in range(4):
        rows_n = slice(n * 64, (n + 1) * 64)
        u = zbuf[rows_n]
        inner = jnp.sum(u * per_u, axis=1, keepdims=True)
        gz[rows_n] = ((per_u - u * inner) * rzbuf[rows_n]).astype(BF)

    to_gx = copy(gz.at[:, half(other)], gx, sibling)

    def rows_of(core, j):
        return jnp.concatenate([tt[core, px, py] for px, py in [place(j, m) for m in range(4)]], axis=0)

    low, high = pl.ds(0, 2), pl.ds(2, 2)
    g_own = gz[:, half(k)]
    chunk = {d: (first + d) % 4 for d in range(4)}
    for d in (2, 1, 3, 0):
        v = jnp.dot(rows_of(k, chunk[d]), g_own, preferred_element_type=F32)
        if d == 2:
            to_gx.wait_recv()
            g_other = gx[...]
        v = v + jnp.dot(rows_of(other, chunk[d]), g_other, preferred_element_type=F32)
        hs[chunk[d]] = v.astype(BF).reshape(4, 80, 640)
        if d == 2:
            via_up = copy(hs.at[chunk[2], low], hr.at[0], to_first(1))
            via_down = copy(hs.at[chunk[2], high], hr.at[1], to_first(3))
        elif d == 1:
            own_up = copy(hs.at[chunk[1], high], hr.at[2], to_first(1))
        elif d == 3:
            own_down = copy(hs.at[chunk[3], low], hr.at[3], to_first(3))

    def grad_tpl(m):
        v = 0.0
        for h in range(2):
            w = pf[h, m].reshape(320, 640)
            v = v + lax.dot_general(
                gz[:, h * 640:(h + 1) * 640], w, (((1,), (1,)), ((), ())), preferred_element_type=F32)
        gt_out[:, m * 320:(m + 1) * 320] = v.astype(BF)

    grad_tpl(0)
    grad_tpl(1)
    via_up.wait_recv()
    hc[0] = (hs[chunk[1], low].astype(F32) + hr[0].astype(F32)).astype(BF)
    sum_up = copy(hc.at[0], hr.at[4], to_first(1))
    via_down.wait_recv()
    hc[1] = (hs[chunk[3], high].astype(F32) + hr[1].astype(F32)).astype(BF)
    sum_down = copy(hc.at[1], hr.at[5], to_first(3))
    grad_tpl(2)
    grad_tpl(3)
    stores = [
        pltpu.make_async_copy(gt_out.at[pl.ds(128 * n, 128)], dst, store_sem.at[n])
        for n, dst in enumerate((gt_low, gt_high))
    ]
    for store in stores:
        store.start()
    for part, direct, summed, a, b in ((low, own_down, sum_up, 3, 4), (high, own_up, sum_down, 2, 5)):
        direct.wait_recv()
        summed.wait_recv()
        own = hs[first, part].astype(F32) + hr[a].astype(F32) + hr[b].astype(F32)
        h2[part] = own.astype(BF)
    got = [copy(h2.at[(second + d) % 4], h2r.at[d - 1], to_second(d)) for d in (2, 1, 3)]
    for cp in got:
        cp.wait_recv()
    own = h2[second].astype(F32)
    for d in range(3):
        own = own + h2r[d].astype(F32)
    rs[...] = own.astype(BF)

    def block_copy(j):
        ahead = (4 * k + j + 12 - c) % 8
        near = z + ahead - 8 * (ahead // 5)
        slot = (ahead + 6) % 7
        return ahead, pltpu.make_async_remote_copy(
            src_ref=rs.at[:, pl.ds(128 * j, 256)], dst_ref=w_recv.at[slot],
            send_sem=w_send.at[j], recv_sem=w_recv_sem.at[slot],
            device_id=to_z(near, k), device_id_type=MESH)

    for j in range(4):
        ahead_j, cp = block_copy(j)

        @pl.when(ahead_j != 0)
        def _():
            cp.start()

    def final_copy(n, core, py):
        return pltpu.make_async_remote_copy(
            src_ref=hp, dst_ref=hy.at[y % 2], send_sem=y_send.at[n], recv_sem=y_recv.at[y % 2],
            device_id=device(x, core, py, zh, c), device_id_type=MESH)

    def four_copy(n):
        return pltpu.make_async_remote_copy(
            src_ref=h_send, dst_ref=h_recv.at[n], send_sem=w_send.at[4 + n], recv_sem=w_recv_sem.at[7 + n],
            device_id=to_z(z + 4 - 8 * n, k), device_id_type=MESH)

    @pl.when(k != col_core)
    def _():
        own = rs[:, pl.ds(pl.multiple_of(128 * (c % 4), 128), 256)].astype(F32)
        for n in range(7):
            pltpu.make_async_remote_copy(
                src_ref=h_send, dst_ref=w_recv.at[n], send_sem=w_send.at[0], recv_sem=w_recv_sem.at[n],
                device_id=sibling, device_id_type=MESH).wait_recv()
            own = own + w_recv[n].astype(F32)
        h_send[...] = own.astype(BF)
        for n in range(2):
            four_copy(n).start()
        for n in range(2):
            four_copy(n).wait_send()

    @pl.when(k == col_core)
    def _():
        for n in range(2):
            four_copy(n).wait_recv()
        whole = h_recv[0].astype(F32) + h_recv[1].astype(F32)
        hp[...] = pltpu.roll(whole, (256 - 32 * (c % 4)) % 256, 1).astype(BF)
        for d in (2, 1, 3):
            final_copy(d, row_core, (y + d) % 4).start()

        @pl.when(k != row_core)
        def _():
            final_copy(0, row_core, y).start()

        @pl.when(k == row_core)
        def _():
            hy[y % 2] = hp[...]

    for n in range(2):
        @pl.when(jnp.logical_or(2 * k + n != y, k != col_core))
        def _():
            pltpu.make_async_remote_copy(
                src_ref=hp, dst_ref=hy.at[n], send_sem=y_send.at[0], recv_sem=y_recv.at[n],
                device_id=sibling, device_id_type=MESH).wait_recv()
        gp_out[80 * n:80 * n + 80] = hy[n, :, 0:160].astype(F32)

    for j in range(4):
        ahead_j, cp = block_copy(j)

        @pl.when(ahead_j != 0)
        def _():
            cp.wait_send()

    @pl.when(k == col_core)
    def _():
        for d in (2, 1, 3):
            final_copy(d, row_core, (y + d) % 4).wait_send()

        @pl.when(k != row_core)
        def _():
            final_copy(0, row_core, y).wait_send()
    for store in stores:
        store.wait()
    copy.finish()


def body(images, labels, templates, projection):
    flat = templates.reshape(256, 1280)
    vm = pl.BlockSpec(memory_space=pltpu.VMEM)
    hbm = pl.BlockSpec(memory_space=pl.ANY)
    scratch = [
        ((256, 1280), BF),
        ((256, 1280), BF), ((256, 1280), BF), ((160, 160), BF),
        ((80, 256), F32), ((80, 256), BF), ((4, 80, 256), BF), ((2, 4, 4, 80, 640), BF),
        ((2, 4, 4, 80, 256), BF), ((256, 1280), F32), ((256, 1), F32),
        ((4, 16, 1280), BF), ((3, 16, 1280), BF), ((16, 1280), BF), ((2, 16, 1280), BF),
        ((4, 4, 16, 1280), BF), ((16, 1280), BF), ((256, 1280), BF), ((2, 256, 1280), BF),
        ((2, 1, 256), jnp.int32), ((256, 512), F32), ((1, 512), F32), ((15, 1, 512), F32),
        ((256, 512), BF), ((2, 4, 4, 16, 640), BF), ((2, 3, 4, 16, 640), BF), ((2, 4, 16, 640), BF),
        ((2, 3, 16, 640), BF), ((16, 1280), BF), ((2, 16, 1280), BF),
        ((4, 16, 1280), BF), ((256, 1280), BF), ((256, 640), BF),
        ((4, 4, 80, 640), BF), ((6, 2, 80, 640), BF), ((2, 2, 80, 640), BF), ((4, 80, 640), BF), ((3, 80, 640), BF),
        ((80, 640), BF), ((7, 80, 256), BF), ((80, 256), BF), ((2, 80, 256), BF), ((80, 256), BF),
        ((2, 80, 256), BF),
    ]
    sems = (4, 2, N_COPIES, N_COPIES, 9, 5, 6, 9, 4, 2)
    gt_low, gt_high, gp = pl.pallas_call(
        kernel,
        out_shape=(jax.ShapeDtypeStruct((128, 1280), BF),) * 2 + (jax.ShapeDtypeStruct((160, 160), F32),),
        in_specs=[hbm] * 4,
        out_specs=(hbm, hbm, vm),
        scratch_shapes=[pltpu.VMEM(s, d) for s, d in scratch]
        + [pltpu.SemaphoreType.DMA((n,)) for n in sems],
        compiler_params=pltpu.CompilerParams(
            collective_id=0, has_side_effects=True, vmem_limit_bytes=60 << 20),
    )(images, labels.reshape(1, 256), flat, projection)
    gt = jnp.concatenate([gt_low, gt_high], axis=0)
    return gt.reshape(templates.shape), gp


def solution(mesh):
    in_specs = (
        P(("img", "tpl"), None),
        P(("img", "tpl")),
        P("tpl", ("cls", "img"), None),
        P("img", "cls"),
    )
    out_specs = (P("tpl", ("cls", "img"), None), P("img", "cls"))
    return jax.shard_map(body, mesh=mesh, in_specs=in_specs, out_specs=out_specs, check_vma=False)
```

```python
import jax
import jax.numpy as jnp
from jax import lax
from jax.experimental import pallas as pl
from jax.experimental.pallas import tpu as pltpu
from jax.sharding import PartitionSpec as P

SCALE = 50.0
EPS = 1e-06
TPL = 32
MESH = pl.DeviceIdType.MESH
BF = jnp.bfloat16
F32 = jnp.float32
PLANE = [(a, b) for a in range(4) for b in range(4) if (a, b) != (0, 0)]
RING = (4, -4, 3, -3, 2, -2, 1, -1)


def inv_norm(v):
    return lax.rsqrt(jnp.sum(v * v, axis=-1, keepdims=True) + EPS)


def device(x, k, y, zh, zl):
    return (x * 2 + k, zl, zh * 4 + y)


class Copies:
    def __init__(self, send, recv):
        self.send, self.recv, self.used = send, recv, 0
        self.open = []

    def __call__(self, src, dst, to):
        n = self.used
        self.used += 1
        cp = pltpu.make_async_remote_copy(
            src_ref=src, dst_ref=dst, send_sem=self.send.at[n], recv_sem=self.recv.at[n],
            device_id=to, device_id_type=MESH)
        cp.start()
        self.open.append(cp)
        return cp

    def finish(self):
        for cp in self.open:
            cp.wait_send()


N_COPIES = 200


def kernel(images_in, labels_in, tpl_in, proj_in, gt_low, gt_high, gp_out,
           gt_out, images, tpl, proj, wf, pw, zb, pf, tt, zbuf, rzbuf, s_send, s_recv, c_send, c_recv, mbuf, mo, cb,
           img, lab, ebuf, e_send, e_recv, gbuf, cg_send, cg_recv, f2, f2r, f_send, f_recv, gs, gz, gx,
           hs, hr, hc, h2, h2r, rs, w_recv, h_send, h_recv, hp, hy,
           load_sem, store_sem, send_sem, recv_sem, z_send, z_recv, w_send, w_recv_sem, y_send, y_recv):
    i = lax.axis_index("img")
    c = lax.axis_index("cls")
    t = lax.axis_index("tpl")
    x, k, y, zh = i // 2, i % 2, t % 4, t // 4
    z = zh * 8 + c
    other = 1 - k
    row_core, col_core = y // 2, c // 4

    def at_plane(dx, dy):
        return (x + dx) % 4, (y + dy) % 4

    def to_plane(dx, dy):
        px, py = at_plane(dx, dy)
        return device(px, k, py, zh, c)

    def to_z(n, core):
        n = (n + 16) % 16
        return device(x, core, y, n // 8, n % 8)

    def to_first(d):
        return device((x + d * other) % 4, k, (y + d * k) % 4, zh, c)

    def to_second(d):
        return device((x + d * k) % 4, k, (y + d * other) % 4, zh, c)

    def place(first, second):
        return first * other + second * k, second * other + first * k

    first, second = place(x, y)
    sibling = device(x, other, y, zh, c)

    barrier = pltpu.get_barrier_semaphore()
    peers = [to_plane(dx, dy) for dx, dy in PLANE]
    peers += [to_z(z + d, k) for d in RING]
    peers += [to_z(z + d, other) for d in RING]
    peers += [device(x, other, (y + d) % 4, zh, c) for d in range(4)]
    for peer in peers:
        pl.semaphore_signal(barrier, inc=1, device_id=peer, device_id_type=MESH)

    loads = [
        pltpu.make_async_copy(src, dst, load_sem.at[n])
        for n, (src, dst) in enumerate(
            ((proj_in, proj), (tpl_in, tpl), (images_in, images), (labels_in, lab.at[k])))
    ]
    for load in loads:
        load.start()

    copy = Copies(send_sem, recv_sem)

    wf[...] = jnp.zeros_like(wf)
    loads[0].wait()
    wf[:, 0:160] = proj[pl.ds(pl.multiple_of(80 * (y % 2), 16), 80), :].astype(F32)
    pw[...] = pltpu.roll(wf[...], 32 * (c % 4), 1).astype(BF)

    pl.semaphore_wait(barrier, len(peers))

    def col_copy(n, d, to, slot=None):
        rows = pl.ds(0, 48) if d == 4 else pl.ds(48, 32) if d == -4 else pl.ds(0, 80)
        slot = c % 4 if slot is None else slot
        return pltpu.make_async_remote_copy(
            src_ref=pw.at[rows], dst_ref=zb.at[slot, rows], send_sem=z_send.at[n],
            recv_sem=z_recv.at[4 if d == -4 else slot], device_id=to, device_id_type=MESH)

    @pl.when(k == row_core)
    def _():
        for n, d in enumerate(RING):
            col_copy(n, d, to_z(z + d, col_core)).start()

        @pl.when(k != col_core)
        def _():
            col_copy(8, 0, sibling).start()

        @pl.when(k == col_core)
        def _():
            zb[c % 4] = pw[...]

    for j in range(4):
        block = 4 * k + j

        @pl.when(block == (c + 4) % 8)
        def _():
            col_copy(0, 4, sibling, j).wait_recv()
            col_copy(0, -4, sibling, j).wait_recv()

        @pl.when(jnp.logical_and(block != (c + 4) % 8, jnp.logical_or(block != c, k != row_core)))
        def _():
            col_copy(0, 0, sibling, j).wait_recv()

    @pl.when(k == row_core)
    def _():
        for n, d in enumerate(RING):
            col_copy(n, d, to_z(z + d, col_core)).wait_send()

        @pl.when(k != col_core)
        def _():
            col_copy(8, 0, sibling).wait_send()
    tiles = [
        zb[0, :, 0:128],
        zb[0, :, 128:256] + zb[1, :, 0:128],
        zb[1, :, 128:256] + zb[2, :, 0:128],
        zb[2, :, 128:256] + zb[3, :, 0:128],
        zb[3, :, 128:256],
    ]
    for j, tile in enumerate(tiles):
        pf[k, x, y, :, j * 128:(j + 1) * 128] = tile

    def piece(d1, d2):
        px, py = place((first + d1) % 4, (second + d2) % 4)
        return pf.at[k, px, py]

    def send(d1, d2, to):
        return copy(piece(d1, d2), piece(d1, d2), to)

    shared = []
    ahead = {d: send(0, 0, to_first(d)) for d in (1, 3, 2)}
    up, down = {}, {}
    for d1 in (0, 3, 1, 2):
        if d1:
            ahead[(4 - d1) % 4].wait_recv()
        up[d1] = send(d1, 0, to_second(1))
        down[d1] = send(d1, 0, to_second(3))
        shared.append(send(d1, 0, sibling))
    for load in loads[1:]:
        load.wait()
    tt[k] = tpl[...].T.reshape(4, 4, 80, 256)
    img_f = images[...].astype(F32)
    img[k] = (img_f * inv_norm(img_f)).astype(BF)
    to_img = copy(img.at[k], img.at[k], sibling)
    to_lab = copy(lab.at[k], lab.at[k], sibling)
    to_tx = copy(tt.at[k], tt.at[k], sibling)

    far = {}
    for d1 in (0, 3, 1, 2):
        up[d1].wait_recv()
        if d1 in (0, 3):
            far[d1] = send(d1, 3, to_second(1))
        down[d1].wait_recv()
        if d1 in (1, 2):
            far[d1] = send(d1, 1, to_second(3))
        shared.append(send(d1, 3, sibling))
        shared.append(send(d1, 1, sibling))
    for d1 in (0, 1, 3, 2):
        far[d1].wait_recv()
        shared.append(send(d1, 2, sibling))

    def half(core):
        return pl.ds(pl.multiple_of(640 * core, 128), 640)

    def project(core):
        zbuf[:, half(core)] = jnp.dot(tpl[...], pf[core].reshape(1280, 640), preferred_element_type=F32)

    project(k)
    for cp in shared:
        cp.wait_recv()
    project(other)
    rz = inv_norm(zbuf[...])
    rzbuf[...] = rz
    zbuf[...] = zbuf[...] * rz
    total = zbuf[0:64] + zbuf[64:128] + zbuf[128:192] + zbuf[192:256]
    s_send[...] = total.astype(BF).reshape(4, 16, 1280)

    halves = [pl.ds(0, 640), pl.ds(640, 640)]
    got = [
        [copy(s_send.at[(y + d) % 4, :, h], s_recv.at[d - 1, :, h], to_plane(0, d)) for d in (2, 1, 3)]
        for h in halves
    ]
    four = []
    for n, h in enumerate(halves):
        for cp in got[n]:
            cp.wait_recv()
        own = s_send[y, :, h].astype(F32)
        for d in range(3):
            own = own + s_recv[d, :, h].astype(F32)
        c_send[:, h] = own.astype(BF)
        four.append([
            copy(c_send.at[:, h], c_recv.at[0, :, h], to_z(z + 4, k)),
            copy(c_send.at[:, h], c_recv.at[1, :, h], to_z(z - 4, k))])

    def mean_piece(d1, h):
        px, py = place((first + d1) % 4, second)
        return mbuf.at[px, py, :, h]

    ahead, wide, back = [], [], []
    for n, h in enumerate(halves):
        for cp in four[n]:
            cp.wait_recv()
        mbuf[x, y, :, h] = ((c_recv[0, :, h].astype(F32) + c_recv[1, :, h].astype(F32)) / TPL).astype(BF)
        src = mean_piece(0, h)
        ahead.append({d: copy(src, src, to_first(d)) for d in (2, 1, 3)})
        wide += [copy(src, src, to_second(d)) for d in (2, 1, 3)]
        back.append(copy(src, mo.at[:, h], to_z(z + 4 - 8 * n, k)))
    for n, h in enumerate(halves):
        for d in (3, 1, 2):
            ahead[n][d].wait_recv()
            src = mean_piece(4 - d, h)
            wide += [copy(src, src, to_second(e)) for e in (2, 1, 3)]
    to_img.wait_recv()
    to_lab.wait_recv()
    to_tx.wait_recv()
    for cp in wide:
        cp.wait_recv()
    mean = mbuf[...].reshape(256, 1280).astype(F32)
    cb[...] = (mean * inv_norm(mean)).astype(BF)
    for s in range(2):
        sc = lax.dot_general(cb[...], img[s], (((1,), (1,)), ((), ())), preferred_element_type=F32)
        ebuf[:, s * 256:(s + 1) * 256] = jnp.exp(SCALE * sc)
    e_send[...] = jnp.sum(ebuf[...], axis=0, keepdims=True)
    got = []
    for d in (4, 3, 5, 2, 6, 1, 7):
        for core in (k, other):
            got.append(copy(e_send, e_recv.at[len(got)], device(x, core, y, zh, (c + d) % 8)))
    got.append(copy(e_send, e_recv.at[14], sibling))
    row = lax.broadcasted_iota(jnp.int32, (256, 1), 0)
    ids = (((c + 4) % 8) * 8 + (row // 64) * 2 + k) * 64 + row % 64
    for cp in got:
        cp.wait_recv()
    tot = e_send[...]
    for n in range(15):
        tot = tot + e_recv[n]
    inv = 1.0 / tot
    for s in range(2):
        part = slice(s * 256, (s + 1) * 256)
        hot = (lab[s, 0:1, :] == ids).astype(F32)
        gbuf[:, part] = (ebuf[:, part] * inv[:, part] - hot).astype(BF)

    got = []
    for n, h in enumerate(halves):
        v = jnp.dot(gbuf[...], img[:, :, h].reshape(512, 640), preferred_element_type=F32)
        cg_send[n] = (SCALE * v).astype(BF).reshape(4, 4, 16, 640)
        got.append([])
        for d in (2, 1, 3):
            for m in range(4):
                px, py = place((first + d) % 4, m)
                got[n].append(copy(cg_send.at[n, px, py], cg_recv.at[n, d - 1, m], to_first(d)))
    step = []
    for n in range(2):
        for cp in got[n]:
            cp.wait_recv()
        for m in range(4):
            px, py = place(first, m)
            own = cg_send[n, px, py].astype(F32)
            for d in range(3):
                own = own + cg_recv[n, d, m].astype(F32)
            f2[n, m] = own.astype(BF)
        step.append([
            copy(f2.at[n, (second + d) % 4], f2r.at[n, d - 1], to_second(d)) for d in (2, 1, 3)])
    four = []
    for n, h in enumerate(halves):
        for cp in step[n]:
            cp.wait_recv()
        own = f2[n, second].astype(F32)
        for d in range(3):
            own = own + f2r[n, d].astype(F32)
        f_send[:, h] = own.astype(BF)
        four += [
            copy(f_send.at[:, h], f_recv.at[0, :, h], to_z(z + 4, k)),
            copy(f_send.at[:, h], f_recv.at[1, :, h], to_z(z - 4, k))]
    for cp in back:
        cp.wait_recv()
    mean = mo[...].astype(F32)
    rn = inv_norm(mean)
    class_w = mean * rn
    for cp in four:
        cp.wait_recv()
    class_g = f_recv[0].astype(F32) + f_recv[1].astype(F32)
    dot_wg = jnp.sum(class_w * class_g, axis=1, keepdims=True)
    gs[y] = ((class_g - class_w * dot_wg) * rn / TPL).astype(BF)
    for cp in [copy(gs.at[y], gs.at[y], to_plane(0, d)) for d in (2, 1, 3)]:
        cp.wait_recv()
    per_u = gs[...].reshape(64, 1280).astype(F32)
    for n in range(4):
        rows_n = slice(n * 64, (n + 1) * 64)
        u = zbuf[rows_n]
        inner = jnp.sum(u * per_u, axis=1, keepdims=True)
        gz[rows_n] = ((per_u - u * inner) * rzbuf[rows_n]).astype(BF)

    to_gx = copy(gz.at[:, half(other)], gx, sibling)

    def rows_of(core, j):
        return jnp.concatenate([tt[core, px, py] for px, py in [place(j, m) for m in range(4)]], axis=0)

    low, high = pl.ds(0, 2), pl.ds(2, 2)
    parts = (pl.ds(0, 48), pl.ds(48, 32))
    via_up, via_down, own_up, own_down, sum_up, sum_down = {}, {}, {}, {}, {}, {}

    def send_via(p):
        r = parts[p]
        via_up[p] = copy(hs.at[chunk[2], low, r], hr.at[0, :, r], to_first(1))
        via_down[p] = copy(hs.at[chunk[2], high, r], hr.at[1, :, r], to_first(3))

    def send_own(p):
        r = parts[p]
        own_up[p] = copy(hs.at[chunk[1], high, r], hr.at[2, :, r], to_first(1))
        own_down[p] = copy(hs.at[chunk[3], low, r], hr.at[3, :, r], to_first(3))

    def send_sum(p):
        r = parts[p]
        via_up[p].wait_recv()
        hc[0, :, r] = (hs[chunk[1], low, r].astype(F32) + hr[0, :, r].astype(F32)).astype(BF)
        sum_up[p] = copy(hc.at[0, :, r], hr.at[4, :, r], to_first(1))
        via_down[p].wait_recv()
        hc[1, :, r] = (hs[chunk[3], high, r].astype(F32) + hr[1, :, r].astype(F32)).astype(BF)
        sum_down[p] = copy(hc.at[1, :, r], hr.at[5, :, r], to_first(3))

    g_own = gz[:, half(k)]
    chunk = {d: (first + d) % 4 for d in range(4)}
    for d in (2, 1, 3, 0):
        v = jnp.dot(rows_of(k, chunk[d]), g_own, preferred_element_type=F32)
        if d == 2:
            to_gx.wait_recv()
            g_other = gx[...]
        v = v + jnp.dot(rows_of(other, chunk[d]), g_other, preferred_element_type=F32)
        hs[chunk[d]] = v.astype(BF).reshape(4, 80, 640)
        if d == 2:
            send_via(0)
        elif d == 3:
            send_own(0)

    def grad_tpl(m):
        v = 0.0
        for h in range(2):
            w = pf[h, m].reshape(320, 640)
            v = v + lax.dot_general(
                gz[:, h * 640:(h + 1) * 640], w, (((1,), (1,)), ((), ())), preferred_element_type=F32)
        gt_out[:, m * 320:(m + 1) * 320] = v.astype(BF)

    grad_tpl(0)
    send_sum(0)
    send_via(1)
    send_own(1)
    grad_tpl(1)
    grad_tpl(2)
    send_sum(1)
    grad_tpl(3)
    stores = [
        pltpu.make_async_copy(gt_out.at[pl.ds(128 * n, 128)], dst, store_sem.at[n])
        for n, dst in enumerate((gt_low, gt_high))
    ]
    for store in stores:
        store.start()
    step = []
    for p, r in enumerate(parts):
        for m, direct, summed, a, b in (
                (low, own_down, sum_up, 3, 4), (high, own_up, sum_down, 2, 5)):
            direct[p].wait_recv()
            summed[p].wait_recv()
            own = hs[first, m, r].astype(F32) + hr[a, :, r].astype(F32) + hr[b, :, r].astype(F32)
            h2[m, r] = own.astype(BF)
        step.append([
            copy(h2.at[(second + d) % 4, r], h2r.at[d - 1, r], to_second(d)) for d in (2, 1, 3)])

    def block_copy(j, p):
        ahead = (4 * k + j + 12 - c) % 8
        near = z + ahead - 8 * ((ahead + p) // 5)
        slot = (ahead + 6) % 7
        return ahead, pltpu.make_async_remote_copy(
            src_ref=rs.at[parts[p], pl.ds(128 * j, 256)], dst_ref=w_recv.at[slot, parts[p]],
            send_sem=w_send.at[2 * j + p], recv_sem=w_recv_sem.at[2 * slot + p],
            device_id=to_z(near, k), device_id_type=MESH)

    for p, r in enumerate(parts):
        for cp in step[p]:
            cp.wait_recv()
        own = h2[second, r].astype(F32)
        for d in range(3):
            own = own + h2r[d, r].astype(F32)
        rs[r] = own.astype(BF)
        for j in range(4):
            ahead_j, cp = block_copy(j, p)

            @pl.when(ahead_j != 0)
            def _():
                cp.start()

    def four_copy(n, p):
        return pltpu.make_async_remote_copy(
            src_ref=h_send.at[parts[p]], dst_ref=h_recv.at[n, parts[p]],
            send_sem=w_send.at[8 + 2 * n + p], recv_sem=w_recv_sem.at[14 + 2 * n + p],
            device_id=to_z(z + 4 - 8 * n, k), device_id_type=MESH)

    def final_copy(n, p, core, py):
        return pltpu.make_async_remote_copy(
            src_ref=hp.at[parts[p]], dst_ref=hy.at[y % 2, parts[p]],
            send_sem=y_send.at[2 * n + p], recv_sem=y_recv.at[2 * (y % 2) + p],
            device_id=device(x, core, py, zh, c), device_id_type=MESH)

    @pl.when(k != col_core)
    def _():
        for p, r in enumerate(parts):
            own = rs[r, pl.ds(pl.multiple_of(128 * (c % 4), 128), 256)].astype(F32)
            for n in range(7):
                pltpu.make_async_remote_copy(
                    src_ref=h_send.at[r], dst_ref=w_recv.at[n, r], send_sem=w_send.at[0],
                    recv_sem=w_recv_sem.at[2 * n + p], device_id=sibling, device_id_type=MESH).wait_recv()
                own = own + w_recv[n, r].astype(F32)
            h_send[r] = own.astype(BF)
            for n in range(2):
                four_copy(n, p).start()
        for p in range(2):
            for n in range(2):
                four_copy(n, p).wait_send()

    @pl.when(k == col_core)
    def _():
        for p, r in enumerate(parts):
            for n in range(2):
                four_copy(n, p).wait_recv()
            whole = h_recv[0, r].astype(F32) + h_recv[1, r].astype(F32)
            hp[r] = pltpu.roll(whole, (256 - 32 * (c % 4)) % 256, 1).astype(BF)
            for d in (2, 1, 3):
                final_copy(d, p, row_core, (y + d) % 4).start()

            @pl.when(k != row_core)
            def _():
                final_copy(0, p, row_core, y).start()

            @pl.when(k == row_core)
            def _():
                hy[y % 2, r] = hp[r]

    for n in range(2):
        @pl.when(jnp.logical_or(2 * k + n != y, k != col_core))
        def _():
            for p, r in enumerate(parts):
                pltpu.make_async_remote_copy(
                    src_ref=hp.at[r], dst_ref=hy.at[n, r], send_sem=y_send.at[0],
                    recv_sem=y_recv.at[2 * n + p], device_id=sibling, device_id_type=MESH).wait_recv()
        gp_out[80 * n:80 * n + 80] = hy[n, :, 0:160].astype(F32)

    for p in range(2):
        for j in range(4):
            ahead_j, cp = block_copy(j, p)

            @pl.when(ahead_j != 0)
            def _():
                cp.wait_send()

    @pl.when(k == col_core)
    def _():
        for p in range(2):
            for d in (2, 1, 3):
                final_copy(d, p, row_core, (y + d) % 4).wait_send()

            @pl.when(k != row_core)
            def _():
                final_copy(0, p, row_core, y).wait_send()
    for store in stores:
        store.wait()
    copy.finish()


def body(images, labels, templates, projection):
    flat = templates.reshape(256, 1280)
    vm = pl.BlockSpec(memory_space=pltpu.VMEM)
    hbm = pl.BlockSpec(memory_space=pl.ANY)
    scratch = [
        ((256, 1280), BF),
        ((256, 1280), BF), ((256, 1280), BF), ((160, 160), BF),
        ((80, 256), F32), ((80, 256), BF), ((4, 80, 256), BF), ((2, 4, 4, 80, 640), BF),
        ((2, 4, 4, 80, 256), BF), ((256, 1280), F32), ((256, 1), F32),
        ((4, 16, 1280), BF), ((3, 16, 1280), BF), ((16, 1280), BF), ((2, 16, 1280), BF),
        ((4, 4, 16, 1280), BF), ((16, 1280), BF), ((256, 1280), BF), ((2, 256, 1280), BF),
        ((2, 1, 256), jnp.int32), ((256, 512), F32), ((1, 512), F32), ((15, 1, 512), F32),
        ((256, 512), BF), ((2, 4, 4, 16, 640), BF), ((2, 3, 4, 16, 640), BF), ((2, 4, 16, 640), BF),
        ((2, 3, 16, 640), BF), ((16, 1280), BF), ((2, 16, 1280), BF),
        ((4, 16, 1280), BF), ((256, 1280), BF), ((256, 640), BF),
        ((4, 4, 80, 640), BF), ((6, 2, 80, 640), BF), ((2, 2, 80, 640), BF), ((4, 80, 640), BF), ((3, 80, 640), BF),
        ((80, 640), BF), ((7, 80, 256), BF), ((80, 256), BF), ((2, 80, 256), BF), ((80, 256), BF),
        ((2, 80, 256), BF),
    ]
    sems = (4, 2, N_COPIES, N_COPIES, 9, 5, 12, 18, 8, 4)
    gt_low, gt_high, gp = pl.pallas_call(
        kernel,
        out_shape=(jax.ShapeDtypeStruct((128, 1280), BF),) * 2 + (jax.ShapeDtypeStruct((160, 160), F32),),
        in_specs=[hbm] * 4,
        out_specs=(hbm, hbm, vm),
        scratch_shapes=[pltpu.VMEM(s, d) for s, d in scratch]
        + [pltpu.SemaphoreType.DMA((n,)) for n in sems],
        compiler_params=pltpu.CompilerParams(
            collective_id=0, has_side_effects=True, vmem_limit_bytes=60 << 20),
    )(images, labels.reshape(1, 256), flat, projection)
    gt = jnp.concatenate([gt_low, gt_high], axis=0)
    return gt.reshape(templates.shape), gp


def solution(mesh):
    in_specs = (
        P(("img", "tpl"), None),
        P(("img", "tpl")),
        P("tpl", ("cls", "img"), None),
        P("img", "cls"),
    )
    out_specs = (P("tpl", ("cls", "img"), None), P("img", "cls"))
    return jax.shard_map(body, mesh=mesh, in_specs=in_specs, out_specs=out_specs, check_vma=False)
```

```python
import jax
import jax.numpy as jnp
from jax import lax
from jax.experimental import pallas as pl
from jax.experimental.pallas import tpu as pltpu
from jax.sharding import PartitionSpec as P

SCALE = 50.0
EPS = 1e-06
TPL = 32
MESH = pl.DeviceIdType.MESH
BF = jnp.bfloat16
F32 = jnp.float32
PLANE = [(a, b) for a in range(4) for b in range(4) if (a, b) != (0, 0)]
RING = (4, -4, 3, -3, 2, -2, 1, -1)


def inv_norm(v):
    return lax.rsqrt(jnp.sum(v * v, axis=-1, keepdims=True) + EPS)


def device(x, k, y, zh, zl):
    return (x * 2 + k, zl, zh * 4 + y)


class Copies:
    def __init__(self, send, recv):
        self.send, self.recv, self.used = send, recv, 0
        self.open = []

    def __call__(self, src, dst, to):
        n = self.used
        self.used += 1
        cp = pltpu.make_async_remote_copy(
            src_ref=src, dst_ref=dst, send_sem=self.send.at[n], recv_sem=self.recv.at[n],
            device_id=to, device_id_type=MESH)
        cp.start()
        self.open.append(cp)
        return cp

    def finish(self):
        for cp in self.open:
            cp.wait_send()


N_COPIES = 200


def kernel(images_in, labels_in, tpl_in, proj_in, gt_low, gt_high, gp_out,
           gt_out, images, tpl, proj, wf, pw, zb, pf, tt, zbuf, rzbuf, s_send, s_recv, c_send, c_recv, mbuf, mo, cb,
           img, lab, ebuf, e_send, e_recv, gbuf, cg_send, cg_recv, f2, f2r, f_send, f_recv, gs, gz, gx,
           hs, hr, hc, h2, h2r, rs, w_recv, h_send, h_recv, hp, hy,
           load_sem, store_sem, send_sem, recv_sem, z_send, z_recv, w_send, w_recv_sem, y_send, y_recv):
    i = lax.axis_index("img")
    c = lax.axis_index("cls")
    t = lax.axis_index("tpl")
    x, k, y, zh = i // 2, i % 2, t % 4, t // 4
    z = zh * 8 + c
    other = 1 - k
    row_core, col_core = y // 2, c // 4

    def at_plane(dx, dy):
        return (x + dx) % 4, (y + dy) % 4

    def to_plane(dx, dy):
        px, py = at_plane(dx, dy)
        return device(px, k, py, zh, c)

    def to_z(n, core):
        n = (n + 16) % 16
        return device(x, core, y, n // 8, n % 8)

    def to_first(d):
        return device((x + d * other) % 4, k, (y + d * k) % 4, zh, c)

    def to_second(d):
        return device((x + d * k) % 4, k, (y + d * other) % 4, zh, c)

    def place(first, second):
        return first * other + second * k, second * other + first * k

    first, second = place(x, y)
    sibling = device(x, other, y, zh, c)

    loads = [
        pltpu.make_async_copy(src, dst, load_sem.at[n])
        for n, (src, dst) in enumerate(
            ((proj_in, proj), (tpl_in, tpl), (images_in, images), (labels_in, lab.at[k])))
    ]
    for load in loads:
        load.start()

    barrier = pltpu.get_barrier_semaphore()
    peers = [to_plane(dx, dy) for dx, dy in PLANE]
    peers += [to_z(z + d, k) for d in RING]
    peers += [to_z(z + d, other) for d in RING]
    peers += [device(x, other, (y + d) % 4, zh, c) for d in range(4)]
    for peer in peers:
        pl.semaphore_signal(barrier, inc=1, device_id=peer, device_id_type=MESH)

    copy = Copies(send_sem, recv_sem)

    wf[...] = jnp.zeros_like(wf)
    loads[0].wait()
    wf[:, 0:160] = proj[pl.ds(pl.multiple_of(80 * (y % 2), 16), 80), :].astype(F32)
    pw[...] = pltpu.roll(wf[...], 32 * (c % 4), 1).astype(BF)

    pl.semaphore_wait(barrier, len(peers))

    def col_copy(n, d, to, slot=None):
        rows = pl.ds(0, 48) if d == 4 else pl.ds(48, 32) if d == -4 else pl.ds(0, 80)
        slot = c % 4 if slot is None else slot
        return pltpu.make_async_remote_copy(
            src_ref=pw.at[rows], dst_ref=zb.at[slot, rows], send_sem=z_send.at[n],
            recv_sem=z_recv.at[4 if d == -4 else slot], device_id=to, device_id_type=MESH)

    @pl.when(k == row_core)
    def _():
        for n, d in enumerate(RING):
            col_copy(n, d, to_z(z + d, col_core)).start()

        @pl.when(k != col_core)
        def _():
            col_copy(8, 0, sibling).start()

        @pl.when(k == col_core)
        def _():
            zb[c % 4] = pw[...]

    for j in range(4):
        block = 4 * k + j

        @pl.when(block == (c + 4) % 8)
        def _():
            col_copy(0, 4, sibling, j).wait_recv()
            col_copy(0, -4, sibling, j).wait_recv()

        @pl.when(jnp.logical_and(block != (c + 4) % 8, jnp.logical_or(block != c, k != row_core)))
        def _():
            col_copy(0, 0, sibling, j).wait_recv()

    @pl.when(k == row_core)
    def _():
        for n, d in enumerate(RING):
            col_copy(n, d, to_z(z + d, col_core)).wait_send()

        @pl.when(k != col_core)
        def _():
            col_copy(8, 0, sibling).wait_send()
    tiles = [
        zb[0, :, 0:128],
        zb[0, :, 128:256] + zb[1, :, 0:128],
        zb[1, :, 128:256] + zb[2, :, 0:128],
        zb[2, :, 128:256] + zb[3, :, 0:128],
        zb[3, :, 128:256],
    ]
    for j, tile in enumerate(tiles):
        pf[k, x, y, :, j * 128:(j + 1) * 128] = tile

    def piece(d1, d2):
        px, py = place((first + d1) % 4, (second + d2) % 4)
        return pf.at[k, px, py]

    def send(d1, d2, to):
        return copy(piece(d1, d2), piece(d1, d2), to)

    shared, far = [], {}
    ahead = {d: send(0, 0, to_first(d)) for d in (1, 3, 2)}
    up, down = {}, {}
    for d1 in (0, 3, 1, 2):
        if d1:
            ahead[(4 - d1) % 4].wait_recv()
        up[d1] = send(d1, 0, to_second(1))
        down[d1] = send(d1, 0, to_second(3))
        if d1 == 2:
            far[d1] = send(d1, 0, to_second(2))
        shared.append(send(d1, 0, sibling))
    for load in loads[1:]:
        load.wait()
    tt[k] = tpl[...].T.reshape(4, 4, 80, 256)
    img_f = images[...].astype(F32)
    img[k] = (img_f * inv_norm(img_f)).astype(BF)
    to_img = copy(img.at[k], img.at[k], sibling)
    to_lab = copy(lab.at[k], lab.at[k], sibling)
    to_tx = copy(tt.at[k], tt.at[k], sibling)

    for d1 in (0, 3, 1, 2):
        up[d1].wait_recv()
        if d1 in (0, 3):
            far[d1] = send(d1, 3, to_second(1))
        down[d1].wait_recv()
        if d1 == 1:
            far[d1] = send(d1, 1, to_second(3))
        shared.append(send(d1, 3, sibling))
        shared.append(send(d1, 1, sibling))
    for d1 in (0, 1, 3, 2):
        far[d1].wait_recv()
        shared.append(send(d1, 2, sibling))

    def half(core):
        return pl.ds(pl.multiple_of(640 * core, 128), 640)

    def project(core):
        zbuf[:, half(core)] = jnp.dot(tpl[...], pf[core].reshape(1280, 640), preferred_element_type=F32)

    project(k)
    for cp in shared:
        cp.wait_recv()
    project(other)
    rz = inv_norm(zbuf[...])
    rzbuf[...] = rz
    zbuf[...] = zbuf[...] * rz
    total = zbuf[0:64] + zbuf[64:128] + zbuf[128:192] + zbuf[192:256]
    s_send[...] = total.astype(BF).reshape(4, 16, 1280)

    halves = [pl.ds(0, 640), pl.ds(640, 640)]
    got = [
        [copy(s_send.at[(y + d) % 4, :, h], s_recv.at[d - 1, :, h], to_plane(0, d)) for d in (2, 1, 3)]
        for h in halves
    ]
    four = []
    for n, h in enumerate(halves):
        for cp in got[n]:
            cp.wait_recv()
        own = s_send[y, :, h].astype(F32)
        for d in range(3):
            own = own + s_recv[d, :, h].astype(F32)
        c_send[:, h] = own.astype(BF)
        four.append([
            copy(c_send.at[:, h], c_recv.at[0, :, h], to_z(z + 4, k)),
            copy(c_send.at[:, h], c_recv.at[1, :, h], to_z(z - 4, k))])

    def mean_piece(d1, h):
        px, py = place((first + d1) % 4, second)
        return mbuf.at[px, py, :, h]

    ahead, wide, back = [], [], []
    for n, h in enumerate(halves):
        for cp in four[n]:
            cp.wait_recv()
        mbuf[x, y, :, h] = ((c_recv[0, :, h].astype(F32) + c_recv[1, :, h].astype(F32)) / TPL).astype(BF)
        src = mean_piece(0, h)
        ahead.append({d: copy(src, src, to_first(d)) for d in (2, 1, 3)})
        wide += [copy(src, src, to_second(d)) for d in (2, 1, 3)]
        back.append(copy(src, mo.at[:, h], to_z(z + 4 - 8 * n, k)))
    for n, h in enumerate(halves):
        for d in (3, 1, 2):
            ahead[n][d].wait_recv()
            src = mean_piece(4 - d, h)
            wide += [copy(src, src, to_second(e)) for e in (2, 1, 3)]
    to_img.wait_recv()
    to_lab.wait_recv()
    to_tx.wait_recv()
    for cp in wide:
        cp.wait_recv()
    mean = mbuf[...].reshape(256, 1280).astype(F32)
    cb[...] = (mean * inv_norm(mean)).astype(BF)
    for s in range(2):
        sc = lax.dot_general(cb[...], img[s], (((1,), (1,)), ((), ())), preferred_element_type=F32)
        ebuf[:, s * 256:(s + 1) * 256] = jnp.exp(SCALE * sc)
    e_send[...] = jnp.sum(ebuf[...], axis=0, keepdims=True)
    got = []
    for d in (4, 3, 5, 2, 6, 1, 7):
        for core in (k, other):
            got.append(copy(e_send, e_recv.at[len(got)], device(x, core, y, zh, (c + d) % 8)))
    got.append(copy(e_send, e_recv.at[14], sibling))
    row = lax.broadcasted_iota(jnp.int32, (256, 1), 0)
    ids = (((c + 4) % 8) * 8 + (row // 64) * 2 + k) * 64 + row % 64
    for cp in got:
        cp.wait_recv()
    tot = e_send[...]
    for n in range(15):
        tot = tot + e_recv[n]
    inv = 1.0 / tot
    for s in range(2):
        part = slice(s * 256, (s + 1) * 256)
        hot = (lab[s, 0:1, :] == ids).astype(F32)
        gbuf[:, part] = (ebuf[:, part] * inv[:, part] - hot).astype(BF)

    got = []
    for n, h in enumerate(halves):
        v = jnp.dot(gbuf[...], img[:, :, h].reshape(512, 640), preferred_element_type=F32)
        cg_send[n] = (SCALE * v).astype(BF).reshape(4, 4, 16, 640)
        got.append([])
        for d in (2, 1, 3):
            for m in range(4):
                px, py = place((first + d) % 4, m)
                got[n].append(copy(cg_send.at[n, px, py], cg_recv.at[n, d - 1, m], to_first(d)))
    step = []
    for n in range(2):
        for cp in got[n]:
            cp.wait_recv()
        for m in range(4):
            px, py = place(first, m)
            own = cg_send[n, px, py].astype(F32)
            for d in range(3):
                own = own + cg_recv[n, d, m].astype(F32)
            f2[n, m] = own.astype(BF)
        step.append([
            copy(f2.at[n, (second + d) % 4], f2r.at[n, d - 1], to_second(d)) for d in (2, 1, 3)])
    four = []
    for n, h in enumerate(halves):
        for cp in step[n]:
            cp.wait_recv()
        own = f2[n, second].astype(F32)
        for d in range(3):
            own = own + f2r[n, d].astype(F32)
        f_send[:, h] = own.astype(BF)
        four += [
            copy(f_send.at[:, h], f_recv.at[0, :, h], to_z(z + 4, k)),
            copy(f_send.at[:, h], f_recv.at[1, :, h], to_z(z - 4, k))]
    for cp in back:
        cp.wait_recv()
    mean = mo[...].astype(F32)
    rn = inv_norm(mean)
    class_w = mean * rn
    for cp in four:
        cp.wait_recv()
    class_g = f_recv[0].astype(F32) + f_recv[1].astype(F32)
    dot_wg = jnp.sum(class_w * class_g, axis=1, keepdims=True)
    gs[y] = ((class_g - class_w * dot_wg) * rn / TPL).astype(BF)
    for cp in [copy(gs.at[y], gs.at[y], to_plane(0, d)) for d in (2, 1, 3)]:
        cp.wait_recv()
    per_u = gs[...].reshape(64, 1280).astype(F32)
    to_gx = []
    for n in range(4):
        rows_n = slice(n * 64, (n + 1) * 64)
        u = zbuf[rows_n]
        inner = jnp.sum(u * per_u, axis=1, keepdims=True)
        gz[rows_n] = ((per_u - u * inner) * rzbuf[rows_n]).astype(BF)
        r = pl.ds(64 * n, 64)
        to_gx.append(copy(gz.at[r, half(other)], gx.at[r], sibling))

    def rows_of(core, j):
        return jnp.concatenate([tt[core, px, py] for px, py in [place(j, m) for m in range(4)]], axis=0)

    low, high = pl.ds(0, 2), pl.ds(2, 2)
    parts = (pl.ds(0, 48), pl.ds(48, 32))
    via_up, via_down, own_up, own_down, sum_up, sum_down = {}, {}, {}, {}, {}, {}

    def send_via(p):
        r = parts[p]
        via_up[p] = copy(hs.at[chunk[2], low, r], hr.at[0, :, r], to_first(1))
        via_down[p] = copy(hs.at[chunk[2], high, r], hr.at[1, :, r], to_first(3))

    def send_own(p):
        r = parts[p]
        own_up[p] = copy(hs.at[chunk[1], high, r], hr.at[2, :, r], to_first(1))
        own_down[p] = copy(hs.at[chunk[3], low, r], hr.at[3, :, r], to_first(3))

    def send_sum(p):
        r = parts[p]
        via_up[p].wait_recv()
        hc[0, :, r] = (hs[chunk[1], low, r].astype(F32) + hr[0, :, r].astype(F32)).astype(BF)
        sum_up[p] = copy(hc.at[0, :, r], hr.at[4, :, r], to_first(1))
        via_down[p].wait_recv()
        hc[1, :, r] = (hs[chunk[3], high, r].astype(F32) + hr[1, :, r].astype(F32)).astype(BF)
        sum_down[p] = copy(hc.at[1, :, r], hr.at[5, :, r], to_first(3))

    g_own = gz[:, half(k)]
    chunk = {d: (first + d) % 4 for d in range(4)}
    for d in (2, 1, 3, 0):
        v = jnp.dot(rows_of(k, chunk[d]), g_own, preferred_element_type=F32)
        if d == 2:
            for cp in to_gx:
                cp.wait_recv()
            g_other = gx[...]
        v = v + jnp.dot(rows_of(other, chunk[d]), g_other, preferred_element_type=F32)
        hs[chunk[d]] = v.astype(BF).reshape(4, 80, 640)
        if d == 2:
            send_via(0)
        elif d == 3:
            send_own(0)

    def grad_tpl(m):
        v = 0.0
        for h in range(2):
            w = pf[h, m].reshape(320, 640)
            v = v + lax.dot_general(
                gz[:, h * 640:(h + 1) * 640], w, (((1,), (1,)), ((), ())), preferred_element_type=F32)
        gt_out[:, m * 320:(m + 1) * 320] = v.astype(BF)

    grad_tpl(0)
    send_sum(0)
    send_via(1)
    send_own(1)
    grad_tpl(1)
    grad_tpl(2)
    send_sum(1)
    grad_tpl(3)
    stores = [
        pltpu.make_async_copy(gt_out.at[pl.ds(128 * n, 128)], dst, store_sem.at[n])
        for n, dst in enumerate((gt_low, gt_high))
    ]
    for store in stores:
        store.start()
    step = []
    for p, r in enumerate(parts):
        for m, direct, summed, a, b in (
                (low, own_down, sum_up, 3, 4), (high, own_up, sum_down, 2, 5)):
            direct[p].wait_recv()
            summed[p].wait_recv()
            own = hs[first, m, r].astype(F32) + hr[a, :, r].astype(F32) + hr[b, :, r].astype(F32)
            h2[m, r] = own.astype(BF)
        step.append([
            copy(h2.at[(second + d) % 4, r], h2r.at[d - 1, r], to_second(d)) for d in (2, 1, 3)])

    def block_copy(j, p):
        ahead = (4 * k + j + 12 - c) % 8
        near = z + ahead - 8 * ((ahead + p) // 5)
        slot = (ahead + 6) % 7
        return ahead, pltpu.make_async_remote_copy(
            src_ref=rs.at[parts[p], pl.ds(128 * j, 256)], dst_ref=w_recv.at[slot, parts[p]],
            send_sem=w_send.at[2 * j + p], recv_sem=w_recv_sem.at[2 * slot + p],
            device_id=to_z(near, k), device_id_type=MESH)

    for p, r in enumerate(parts):
        for cp in step[p]:
            cp.wait_recv()
        own = h2[second, r].astype(F32)
        for d in range(3):
            own = own + h2r[d, r].astype(F32)
        rs[r] = own.astype(BF)
        for j in range(4):
            ahead_j, cp = block_copy(j, p)

            @pl.when(ahead_j != 0)
            def _():
                cp.start()

    def four_copy(n, p):
        return pltpu.make_async_remote_copy(
            src_ref=h_send.at[parts[p]], dst_ref=h_recv.at[n, parts[p]],
            send_sem=w_send.at[8 + 2 * n + p], recv_sem=w_recv_sem.at[14 + 2 * n + p],
            device_id=to_z(z + 4 - 8 * n, k), device_id_type=MESH)

    def final_copy(n, p, core, py):
        return pltpu.make_async_remote_copy(
            src_ref=hp.at[parts[p]], dst_ref=hy.at[y % 2, parts[p]],
            send_sem=y_send.at[2 * n + p], recv_sem=y_recv.at[2 * (y % 2) + p],
            device_id=device(x, core, py, zh, c), device_id_type=MESH)

    @pl.when(k != col_core)
    def _():
        for p, r in enumerate(parts):
            own = rs[r, pl.ds(pl.multiple_of(128 * (c % 4), 128), 256)].astype(F32)
            for n in range(7):
                pltpu.make_async_remote_copy(
                    src_ref=h_send.at[r], dst_ref=w_recv.at[n, r], send_sem=w_send.at[0],
                    recv_sem=w_recv_sem.at[2 * n + p], device_id=sibling, device_id_type=MESH).wait_recv()
                own = own + w_recv[n, r].astype(F32)
            h_send[r] = own.astype(BF)
            for n in range(2):
                four_copy(n, p).start()
        for p in range(2):
            for n in range(2):
                four_copy(n, p).wait_send()

    @pl.when(k == col_core)
    def _():
        for p, r in enumerate(parts):
            for n in range(2):
                four_copy(n, p).wait_recv()
            whole = h_recv[0, r].astype(F32) + h_recv[1, r].astype(F32)
            hp[r] = pltpu.roll(whole, (256 - 32 * (c % 4)) % 256, 1).astype(BF)
            for d in (2, 1, 3):
                final_copy(d, p, row_core, (y + d) % 4).start()

            @pl.when(k != row_core)
            def _():
                final_copy(0, p, row_core, y).start()

            @pl.when(k == row_core)
            def _():
                hy[y % 2, r] = hp[r]

    for n in range(2):
        @pl.when(jnp.logical_or(2 * k + n != y, k != col_core))
        def _():
            for p, r in enumerate(parts):
                pltpu.make_async_remote_copy(
                    src_ref=hp.at[r], dst_ref=hy.at[n, r], send_sem=y_send.at[0],
                    recv_sem=y_recv.at[2 * n + p], device_id=sibling, device_id_type=MESH).wait_recv()
        gp_out[80 * n:80 * n + 80] = hy[n, :, 0:160].astype(F32)

    for p in range(2):
        for j in range(4):
            ahead_j, cp = block_copy(j, p)

            @pl.when(ahead_j != 0)
            def _():
                cp.wait_send()

    @pl.when(k == col_core)
    def _():
        for p in range(2):
            for d in (2, 1, 3):
                final_copy(d, p, row_core, (y + d) % 4).wait_send()

            @pl.when(k != row_core)
            def _():
                final_copy(0, p, row_core, y).wait_send()
    for store in stores:
        store.wait()
    copy.finish()


def body(images, labels, templates, projection):
    flat = templates.reshape(256, 1280)
    vm = pl.BlockSpec(memory_space=pltpu.VMEM)
    hbm = pl.BlockSpec(memory_space=pl.ANY)
    scratch = [
        ((256, 1280), BF),
        ((256, 1280), BF), ((256, 1280), BF), ((160, 160), BF),
        ((80, 256), F32), ((80, 256), BF), ((4, 80, 256), BF), ((2, 4, 4, 80, 640), BF),
        ((2, 4, 4, 80, 256), BF), ((256, 1280), F32), ((256, 1), F32),
        ((4, 16, 1280), BF), ((3, 16, 1280), BF), ((16, 1280), BF), ((2, 16, 1280), BF),
        ((4, 4, 16, 1280), BF), ((16, 1280), BF), ((256, 1280), BF), ((2, 256, 1280), BF),
        ((2, 1, 256), jnp.int32), ((256, 512), F32), ((1, 512), F32), ((15, 1, 512), F32),
        ((256, 512), BF), ((2, 4, 4, 16, 640), BF), ((2, 3, 4, 16, 640), BF), ((2, 4, 16, 640), BF),
        ((2, 3, 16, 640), BF), ((16, 1280), BF), ((2, 16, 1280), BF),
        ((4, 16, 1280), BF), ((256, 1280), BF), ((256, 640), BF),
        ((4, 4, 80, 640), BF), ((6, 2, 80, 640), BF), ((2, 2, 80, 640), BF), ((4, 80, 640), BF), ((3, 80, 640), BF),
        ((80, 640), BF), ((7, 80, 256), BF), ((80, 256), BF), ((2, 80, 256), BF), ((80, 256), BF),
        ((2, 80, 256), BF),
    ]
    sems = (4, 2, N_COPIES, N_COPIES, 9, 5, 12, 18, 8, 4)
    gt_low, gt_high, gp = pl.pallas_call(
        kernel,
        out_shape=(jax.ShapeDtypeStruct((128, 1280), BF),) * 2 + (jax.ShapeDtypeStruct((160, 160), F32),),
        in_specs=[hbm] * 4,
        out_specs=(hbm, hbm, vm),
        scratch_shapes=[pltpu.VMEM(s, d) for s, d in scratch]
        + [pltpu.SemaphoreType.DMA((n,)) for n in sems],
        compiler_params=pltpu.CompilerParams(
            collective_id=0, has_side_effects=True, vmem_limit_bytes=60 << 20),
    )(images, labels.reshape(1, 256), flat, projection)
    gt = jnp.concatenate([gt_low, gt_high], axis=0)
    return gt.reshape(templates.shape), gp


def solution(mesh):
    in_specs = (
        P(("img", "tpl"), None),
        P(("img", "tpl")),
        P("tpl", ("cls", "img"), None),
        P("img", "cls"),
    )
    out_specs = (P("tpl", ("cls", "img"), None), P("img", "cls"))
    return jax.shard_map(body, mesh=mesh, in_specs=in_specs, out_specs=out_specs, check_vma=False)
```
